512 devices in a mesh: dp: 32 (over y_hi, z, core), cent: 16 (over y_lo, x).
Axes of the slice: x: 4, y: 8 (y_hi: 2, y_lo: 4; y = y_hi * 4 + y_lo), z: 8, core: 2. Of those that a mesh axis runs over, the one named last changes fastest.
Arguments:
- points: bfloat16 [32768, 1024], P('dp'), may hold values from -64 to 64
- centroids: bfloat16 [12288, 1024], P('cent', 'dp'), may hold values from -50 to 50
- groups: bfloat16 [4096, 1024], P('dp'), may hold values from -50 to 50
Outputs:
- fresh: bfloat16 [12288, 1024], P('cent')
- new_groups: bfloat16 [4096, 1024], P('dp')
The draws below stay inside these ranges and needn't reach their ends.
All inputs are finite; a program needn't handle non-finite values.
Results may differ from the reference program's by a relative error of at most 0.0065.
Values may be sent and summed in bfloat16 or wider, within the bound.
No kernel may reach another device: no remote copies, remote signals or barrier semaphores. Data moves between devices by JAX's collectives and lax.ppermute only.
A program may use at most 64 MiB of HBM per device.

```python
import jax
import jax.numpy as jnp
from jax import lax

D = 1024
PTS_DEV = 1024
K1_DEV = 768
K2 = 4096
NPTS = 32768
K1 = 12288
N_DP = 32
N_CENT = 16


def centroid_table(key):
    table_key = jax.random.fold_in(key, 11)
    stride = K1 // N_DP
    base = jax.random.truncated_normal(table_key, -6.0, 6.0, (K1, D), jnp.float32)
    rows = lax.broadcasted_iota(jnp.int32, (K1, 1), 0)
    enlarge = 64.0 / D ** 0.5
    base = jnp.where(rows % stride == 0, base * enlarge, base)
    twin = jnp.roll(base, 1, axis=0) * 1.02
    return jnp.where(rows % stride == 1, twin, base)


def draw_centroids(key, part):
    table = centroid_table(key)
    return table.astype(jnp.bfloat16)


def draw_points(key, part):
    table = centroid_table(key)
    key = jax.random.fold_in(key, 3)
    stride = K1 // N_DP
    rows = lax.broadcasted_iota(jnp.int32, (NPTS,), 0)
    slab = rows // PTS_DEV
    picked = slab * stride
    factor = 1.1 + 0.1 * (rows // 8 % 3).astype(jnp.float32)
    aligned = table[picked] * factor[:, None]
    noise = jax.random.truncated_normal(key, -6.0, 6.0, (NPTS, D), jnp.float32)
    result = jnp.where((rows % 8 == 5)[:, None], aligned, noise)
    return result.astype(jnp.bfloat16)


def draw_groups(key, part):
    table = centroid_table(key)
    key = jax.random.fold_in(key, 5)
    stride = K1 // N_DP
    key_base = jax.random.fold_in(key, 0)
    key_nudge = jax.random.fold_in(key, 2)
    rows = lax.broadcasted_iota(jnp.int32, (K2,), 0)
    cluster = rows // 64
    target = cluster * stride % K1
    aligned = table[target]
    nudge = jax.random.normal(key_nudge, (K2, D), jnp.float32) * 0.2
    base = jax.random.truncated_normal(key_base, -6.0, 6.0, (K2, D), jnp.float32)
    slot = (rows % 64)[:, None]
    result = jnp.where(slot == 7, aligned, jnp.where(slot == 8, aligned + nudge, base))
    result = jnp.clip(result, -50.0, 50.0)
    return result.astype(jnp.bfloat16)


def setup_inputs(seed: int = 0) -> dict:
    seeds = jax.random.split(jax.random.key(seed), 4)
    points = draw_points(jax.random.fold_in(seeds[3], 71), 0)
    centroids = draw_centroids(jax.random.fold_in(seeds[3], 71), 0)
    groups = draw_groups(jax.random.fold_in(seeds[3], 71), 0)
    return dict(points=points, centroids=centroids, groups=groups)


temper = 20.0


def soft_rows(scores):
    peak_row = jnp.max(scores, axis=1, keepdims=True)
    expo = jnp.exp(scores - peak_row)
    row_total = jnp.sum(expo, axis=1, keepdims=True)
    return (expo / row_total).astype(jnp.bfloat16)


def reference(points, centroids, groups):
    cent_wide = centroids.astype(jnp.float32)
    cnorm = jnp.sum(cent_wide * cent_wide, axis=1)
    point_blocks = points.reshape(N_DP, PTS_DEV, D)

    def level_one(carry, block):
        sums_acc, count_acc = carry
        product = jnp.dot(block, centroids.T, preferred_element_type=jnp.float32)
        scores = (2.0 * product - cnorm[None, :]) / temper
        resp = soft_rows(scores)
        sums_acc = sums_acc + jnp.dot(resp.T, block, preferred_element_type=jnp.float32)
        count_acc = count_acc + jnp.sum(resp.astype(jnp.float32), axis=0)
        return (sums_acc, count_acc), None

    init_one = (jnp.zeros((K1, D), jnp.float32), jnp.zeros((K1,), jnp.float32))
    (sums_one, counts_one), _ = lax.scan(level_one, init_one, point_blocks)
    fresh = ((sums_one + cent_wide) / (counts_one[:, None] + 1.0)).astype(jnp.bfloat16)

    group_wide = groups.astype(jnp.float32)
    gnorm = jnp.sum(group_wide * group_wide, axis=1)

    def level_two(carry, items):
        sums_acc, count_acc = carry
        rows_block, count_block = items
        product = jnp.dot(rows_block, groups.T, preferred_element_type=jnp.float32)
        scores = (2.0 * product - gnorm[None, :]) / temper
        resp = soft_rows(scores)
        weighted = (count_block[:, None] * resp.astype(jnp.float32)).astype(jnp.bfloat16)
        sums_acc = sums_acc + jnp.dot(weighted.T, rows_block, preferred_element_type=jnp.float32)
        count_acc = count_acc + jnp.sum(weighted.astype(jnp.float32), axis=0)
        return (sums_acc, count_acc), None

    init_two = (jnp.zeros((K2, D), jnp.float32), jnp.zeros((K2,), jnp.float32))
    items = (fresh.reshape(N_CENT, K1_DEV, D), counts_one.reshape(N_CENT, K1_DEV))
    (sums_two, counts_two), _ = lax.scan(level_two, init_two, items)
    new_groups = ((sums_two + group_wide) / (counts_two[:, None] + 1.0)).astype(jnp.bfloat16)
    return fresh, new_groups
```

```python
import jax
import jax.numpy as jnp
from jax import lax
from jax.sharding import Mesh, PartitionSpec as P

temper = 20.0
f32, bf16 = jnp.float32, jnp.bfloat16
DP = ("y_hi", "z", "core")
CHIPS = ("y_hi", "z")
CENT = ("y_lo", "x")
SWAP = [(0, 1), (1, 0)]


def spread(block, axes, n):
    return lax.all_to_all(jnp.broadcast_to(block[None], (n, *block.shape)), axes, 0, 0)


def parts(count):
    high = lax.reduce_precision(count, 8, 7)
    rest = count - high
    mid = lax.reduce_precision(rest, 8, 7)
    return [p.astype(bf16) for p in (high, mid, rest - mid)]


def with_count(rows, count):
    n = rows.shape[0]
    lanes = jnp.concatenate([*parts(count), jnp.zeros((n, 125), bf16)], axis=1)
    return jnp.concatenate([rows.astype(bf16), lanes], axis=1)


def add_up(blocks):
    total = jnp.sum(blocks.astype(f32), axis=0)
    count = total[:, 1024:1025] + total[:, 1025:1026] + total[:, 1026:1027]
    return total[:, :1024], count


def combine(peaks, totals):
    peak = jnp.max(peaks, axis=0)
    return peak, jnp.sum(totals * jnp.exp(peaks - peak[None]), axis=0)


def on_device(points, centroids, groups):
    core = lax.axis_index("core")
    chip = lax.axis_index(CHIPS)
    cent = lax.axis_index(CENT)
    points_other = lax.ppermute(points, "core", SWAP)
    groups_other = lax.ppermute(groups, "core", SWAP)
    points_both = jnp.concatenate([points, points_other], axis=0)
    groups_both = jnp.concatenate(
        [
            jnp.where(core == 0, groups, groups_other),
            jnp.where(core == 0, groups_other, groups),
        ],
        axis=0,
    )

    halves = centroids.T.reshape(32, 2, 384).transpose(1, 0, 2)
    to_send = jnp.broadcast_to(halves[None], (16, 2, 32, 384)).reshape(32, 32, 384)
    piece_t = lax.all_to_all(to_send, DP, 0, 0).reshape(1024, 384)
    piece = piece_t.T
    piece_wide = piece.astype(f32)
    norm_one = jnp.sum(piece_wide * piece_wide, axis=1, keepdims=True)
    product_one = lax.dot_general(
        piece, points_both, (((1,), (1,)), ((), ())), preferred_element_type=f32
    )
    scores_one = (2.0 * product_one - norm_one) / temper
    peak_here = jnp.max(scores_one, axis=0)
    total_here = jnp.sum(jnp.exp(scores_one - peak_here[None]), axis=0)
    pairs = spread(jnp.stack([peak_here, total_here]), CENT, 16)
    pair = jnp.stack(combine(pairs[:, 0], pairs[:, 1]))
    other = lax.ppermute(pair, "core", SWAP)
    other = jnp.concatenate([other[:, 1024:], other[:, :1024]], axis=1)
    peak_one, total_one = combine(
        jnp.stack([pair[0], other[0]]), jnp.stack([pair[1], other[1]])
    )
    resp_one = (jnp.exp(scores_one - peak_one[None]) / total_one[None]).astype(bf16)
    sums_one = lax.dot_general(
        resp_one, points_both, (((1,), (0,)), ((), ())), preferred_element_type=f32
    )
    counts_one = jnp.sum(resp_one.astype(f32), axis=1, keepdims=True)
    blocks = with_count(sums_one, counts_one).reshape(16, 24, 1152)
    sums, counts = add_up(lax.all_to_all(blocks, CHIPS, 0, 0))
    piece_rows = lax.dynamic_slice_in_dim(piece, chip * 24, 24, axis=0)
    fresh_rows = ((sums + piece_rows.astype(f32)) / (counts + 1.0)).astype(bf16)
    fresh = spread(fresh_rows, CHIPS, 16).reshape(384, 1024)
    fresh_other = lax.ppermute(fresh, "core", SWAP)
    fresh_all = jnp.concatenate(
        [jnp.where(core == 0, fresh, fresh_other), jnp.where(core == 0, fresh_other, fresh)],
        axis=0,
    )

    group_wide = groups_both.astype(f32)
    norm_two = jnp.sum(group_wide * group_wide, axis=1, keepdims=True)
    product_two = lax.dot_general(
        groups_both, fresh, (((1,), (1,)), ((), ())), preferred_element_type=f32
    )
    scores_two = (2.0 * product_two - norm_two) / temper
    peak_here = jnp.max(scores_two, axis=0)
    total_here = jnp.sum(jnp.exp(scores_two - peak_here[None]), axis=0)
    lane = lax.broadcasted_iota(jnp.int32, (24, 384), 1)
    row = lax.broadcasted_iota(jnp.int32, (24, 384), 0)
    counts_lane = jnp.sum(jnp.where(lane == row + chip * 24, counts, 0.0), axis=0)
    trios = spread(jnp.stack([peak_here, total_here, counts_lane]), CHIPS, 16)
    peak_two, total_two = combine(trios[:, 0], trios[:, 1])
    counts_row = jnp.sum(trios[:, 2], axis=0)
    resp_two = (jnp.exp(scores_two - peak_two[None]) / total_two[None]).astype(bf16)
    weighted = (counts_row[None] * resp_two.astype(f32)).astype(bf16)
    sums_two = lax.dot_general(
        weighted, fresh, (((1,), (0,)), ((), ())), preferred_element_type=f32
    )
    counts_two = jnp.sum(weighted.astype(f32), axis=1, keepdims=True)
    blocks = with_count(sums_two, counts_two).reshape(32, 8, 1152)
    sums, counts = add_up(lax.all_to_all(blocks, ("core", *CENT), 0, 0))
    group_rows = lax.dynamic_slice_in_dim(groups, cent * 8, 8, axis=0)
    new_rows = ((sums + group_rows.astype(f32)) / (counts + 1.0)).astype(bf16)
    new_groups = spread(new_rows, CENT, 16).reshape(128, 1024)
    return (fresh_all, new_groups)


def solution(mesh):
    split = Mesh(mesh.devices.reshape(2, 8, 2, 4, 4), ("y_hi", "z", "core", "y_lo", "x"))
    return jax.shard_map(
        on_device,
        mesh=split,
        in_specs=(P(DP, None), P(CENT, DP), P(DP, None)),
        out_specs=(P(CENT, None), P(DP, None)),
        check_vma=False,
    )
```

```python
import jax
import jax.numpy as jnp
from jax import lax
from jax.experimental import pallas as pl
from jax.experimental.pallas import tpu as pltpu
from jax.sharding import Mesh, PartitionSpec as P

temper = 20.0
f32, bf16 = jnp.float32, jnp.bfloat16
DP = ("y_hi", "z", "core")
CHIPS = ("y_hi", "z")
CENT = ("y_lo", "x")
SWAP = [(0, 1), (1, 0)]
D = 1024
WIDE = 1152
ROWS = 384
OWN = 24
VMEM = pl.BlockSpec(memory_space=pltpu.VMEM)
SMEM = pl.BlockSpec(memory_space=pltpu.SMEM)
NT = (((1,), (1,)), ((), ()))
NN = (((1,), (0,)), ((), ()))


def params():
    return pltpu.CompilerParams(vmem_limit_bytes=40 * 1024 * 1024)


def cost(flops, nbytes, exps=0):
    return pl.CostEstimate(flops=flops, bytes_accessed=nbytes, transcendentals=exps)


def count_lanes(count):
    n = count.shape[0]
    high = count.astype(bf16).astype(f32)
    mid = (count - high).astype(bf16).astype(f32)
    low = count - high - mid
    lane = lax.broadcasted_iota(jnp.int32, (n, 128), 1)
    wide = jnp.where(lane == 0, high, jnp.where(lane == 1, mid, jnp.where(lane == 2, low, 0.0)))
    return wide.astype(bf16)


def add_up(blocks_ref, n):
    total = blocks_ref[0].astype(f32)
    for i in range(1, n):
        total = total + blocks_ref[i].astype(f32)
    count = jnp.sum(total[:, D:], axis=1, keepdims=True)
    return total[:, :D], count


def scores_kernel(piece_t, points_a, points_b, piece, scores_a, scores_b, pairs, norm):
    @pl.when(pl.program_id(0) == 0)
    def _():
        rows = piece_t[...].T
        piece[...] = rows
        wide = rows.astype(f32)
        norm[...] = jnp.sum(wide * wide, axis=1, keepdims=True)

    found = []
    for points, scores in ((points_a, scores_a), (points_b, scores_b)):
        product = lax.dot_general(piece[...], points[...], NT, preferred_element_type=f32)
        s = (2.0 * product - norm[...]) / temper
        scores[...] = s
        peak = jnp.max(s, axis=0, keepdims=True)
        found += [peak, jnp.sum(jnp.exp(s - peak), axis=0, keepdims=True)]
    block = jnp.concatenate(found, axis=0)
    for i in range(16):
        pairs[i] = block


def level_one_scores(piece_t, points_a, points_b):
    step = 256
    points_spec = pl.BlockSpec((step, D), lambda i: (i, 0))
    scores_spec = pl.BlockSpec((ROWS, step), lambda i: (0, i))
    return pl.pallas_call(
        scores_kernel,
        grid=(1024 // step,),
        in_specs=[pl.BlockSpec((D, ROWS), lambda i: (0, 0)), points_spec, points_spec],
        out_specs=[
            pl.BlockSpec((ROWS, D), lambda i: (0, 0)),
            scores_spec,
            scores_spec,
            pl.BlockSpec((16, 4, step), lambda i: (0, 0, i)),
        ],
        out_shape=[
            jax.ShapeDtypeStruct((ROWS, D), bf16),
            jax.ShapeDtypeStruct((ROWS, 1024), f32),
            jax.ShapeDtypeStruct((ROWS, 1024), f32),
            jax.ShapeDtypeStruct((16, 4, 1024), f32),
        ],
        scratch_shapes=[pltpu.VMEM((ROWS, 1), f32)],
        compiler_params=params(),
        cost_estimate=cost(2 * ROWS * 2048 * D, 8 << 20, ROWS * 2048),
    )(piece_t, points_a, points_b)


def combine_kernel(pairs, out):
    for row in (0, 2):
        peaks, totals = pairs[:, row, :], pairs[:, row + 1, :]
        peak = jnp.max(peaks, axis=0, keepdims=True)
        out[row : row + 1, :] = peak
        out[row + 1 : row + 2, :] = jnp.sum(
            totals * jnp.exp(peaks - peak), axis=0, keepdims=True
        )


def combine(pairs):
    return pl.pallas_call(
        combine_kernel,
        in_specs=[VMEM],
        out_specs=VMEM,
        out_shape=jax.ShapeDtypeStruct((4, 1024), f32),
        compiler_params=params(),
        cost_estimate=cost(1 << 17, 1 << 18, 1 << 15),
    )(pairs)


def sums_kernel(mine, other, scores_a, scores_b, points_a, points_b, out, total, count):
    @pl.when(pl.program_id(0) == 0)
    def _():
        total[...] = jnp.zeros_like(total)
        count[...] = jnp.zeros_like(count)

    for at, points, scores in ((0, points_a, scores_a), (2, points_b, scores_b)):
        peak_m, total_m = mine[at : at + 1, :], mine[at + 1 : at + 2, :]
        peak_o, total_o = other[2 - at : 3 - at, :], other[3 - at : 4 - at, :]
        peak = jnp.maximum(peak_m, peak_o)
        whole = total_m * jnp.exp(peak_m - peak) + total_o * jnp.exp(peak_o - peak)
        resp = (jnp.exp(scores[...] - peak) * (1.0 / whole)).astype(bf16)
        total[...] += lax.dot_general(resp, points[...], NN, preferred_element_type=f32)
        count[...] += jnp.sum(resp.astype(f32), axis=1, keepdims=True)

    @pl.when(pl.program_id(0) == pl.num_programs(0) - 1)
    def _():
        out[:, :D] = total[...].astype(bf16)
        out[:, D:] = count_lanes(count[...])


def level_one_sums(mine, other, scores_a, scores_b, points_a, points_b):
    step = 512
    pair_spec = pl.BlockSpec((4, step), lambda i: (0, i))
    points_spec = pl.BlockSpec((step, D), lambda i: (i, 0))
    scores_spec = pl.BlockSpec((ROWS, step), lambda i: (0, i))
    return pl.pallas_call(
        sums_kernel,
        grid=(1024 // step,),
        in_specs=[pair_spec, pair_spec, scores_spec, scores_spec, points_spec, points_spec],
        out_specs=pl.BlockSpec((ROWS, WIDE), lambda i: (0, 0)),
        out_shape=jax.ShapeDtypeStruct((ROWS, WIDE), bf16),
        scratch_shapes=[pltpu.VMEM((ROWS, D), f32), pltpu.VMEM((ROWS, 1), f32)],
        compiler_params=params(),
        cost_estimate=cost(2 * ROWS * 2048 * D, 8 << 20, ROWS * 2048),
    )(mine, other, scores_a, scores_b, points_a, points_b)


def fresh_kernel(chip, blocks, rows, fresh, counts):
    sums, count = add_up(blocks, 16)
    new = ((sums + rows[...].astype(f32)) / (count + 1.0)).astype(bf16)
    for i in range(16):
        fresh[i] = new
    lane = lax.broadcasted_iota(jnp.int32, (OWN, ROWS), 1)
    row = lax.broadcasted_iota(jnp.int32, (OWN, ROWS), 0)
    placed = jnp.where(lane == row + chip[0] * OWN, count, 0.0)
    counts[...] = jnp.sum(placed, axis=0, keepdims=True)


def finish_rows(chip, blocks, rows):
    return pl.pallas_call(
        fresh_kernel,
        in_specs=[SMEM, VMEM, VMEM],
        out_specs=[VMEM, VMEM],
        out_shape=[
            jax.ShapeDtypeStruct((16, OWN, D), bf16),
            jax.ShapeDtypeStruct((1, ROWS), f32),
        ],
        compiler_params=params(),
        cost_estimate=cost(1 << 19, 1 << 20),
    )(chip, blocks, rows)


def group_scores_kernel(fresh, groups, counts, scores, trios):
    wide = groups[...].astype(f32)
    norm = jnp.sum(wide * wide, axis=1, keepdims=True)
    product = lax.dot_general(groups[...], fresh[...], NT, preferred_element_type=f32)
    s = (2.0 * product - norm) / temper
    scores[...] = s
    peak = jnp.max(s, axis=0, keepdims=True)
    total = jnp.sum(jnp.exp(s - peak), axis=0, keepdims=True)
    block = jnp.concatenate([peak, total, counts[...], jnp.zeros_like(peak)], axis=0)
    for i in range(16):
        trios[i] = block


def level_two_scores(fresh, groups, counts):
    return pl.pallas_call(
        group_scores_kernel,
        in_specs=[VMEM] * 3,
        out_specs=[VMEM] * 2,
        out_shape=[
            jax.ShapeDtypeStruct((256, ROWS), f32),
            jax.ShapeDtypeStruct((16, 4, ROWS), f32),
        ],
        compiler_params=params(),
        cost_estimate=cost(2 * ROWS * 256 * D, 2 << 20, ROWS * 256),
    )(fresh, groups, counts)


def group_sums_kernel(scores, trios, fresh, out):
    peaks, totals = trios[:, 0, :], trios[:, 1, :]
    peak = jnp.max(peaks, axis=0, keepdims=True)
    whole = jnp.sum(totals * jnp.exp(peaks - peak), axis=0, keepdims=True)
    counts = jnp.sum(trios[:, 2, :], axis=0, keepdims=True)
    resp = (jnp.exp(scores[...] - peak) * (1.0 / whole)).astype(bf16)
    weighted = (counts * resp.astype(f32)).astype(bf16)
    sums = lax.dot_general(weighted, fresh[...], NN, preferred_element_type=f32)
    out[:, :D] = sums.astype(bf16)
    out[:, D:] = count_lanes(jnp.sum(weighted.astype(f32), axis=1, keepdims=True))


def level_two_sums(scores, trios, fresh):
    return pl.pallas_call(
        group_sums_kernel,
        in_specs=[VMEM] * 3,
        out_specs=VMEM,
        out_shape=jax.ShapeDtypeStruct((256, WIDE), bf16),
        compiler_params=params(),
        cost_estimate=cost(2 * ROWS * 256 * D, 2 << 20, ROWS * 256),
    )(scores, trios, fresh)


def groups_kernel(blocks, rows, out):
    sums, count = add_up(blocks, 32)
    new = ((sums + rows[...].astype(f32)) / (count + 1.0)).astype(bf16)
    for i in range(16):
        out[i] = new


def finish_groups(blocks, rows):
    return pl.pallas_call(
        groups_kernel,
        in_specs=[VMEM] * 2,
        out_specs=VMEM,
        out_shape=jax.ShapeDtypeStruct((16, 8, D), bf16),
        compiler_params=params(),
        cost_estimate=cost(1 << 19, 1 << 20),
    )(blocks, rows)


def exchange(blocks, axes):
    return lax.all_to_all(blocks, axes, 0, 0)


def in_core_order(core, mine, other):
    first = jnp.where(core == 0, mine, other)
    second = jnp.where(core == 0, other, mine)
    return jnp.concatenate([first, second], axis=0)


def on_device(points, centroids, groups):
    core = lax.axis_index("core")
    chip = lax.axis_index(CHIPS)
    cent = lax.axis_index(CENT)

    columns = centroids.T
    target = lax.broadcasted_iota(jnp.int32, (32, 1, 1), 0) % 2
    to_send = jnp.where(target == 0, columns[None, :, :ROWS], columns[None, :, ROWS:])
    piece_t = exchange(to_send, DP).reshape(D, ROWS)
    points_other = lax.ppermute(points, "core", SWAP)
    groups_other = lax.ppermute(groups, "core", SWAP)
    groups_both = in_core_order(core, groups, groups_other)

    piece, scores_a, scores_b, pairs = level_one_scores(piece_t, points, points_other)
    mine = combine(exchange(pairs, CENT))
    other = lax.ppermute(mine, "core", SWAP)
    sums = level_one_sums(mine, other, scores_a, scores_b, points, points_other)
    blocks = exchange(sums.reshape(16, OWN, WIDE), CHIPS)
    rows = lax.dynamic_slice_in_dim(piece, chip * OWN, OWN, axis=0)
    fresh_rows, counts = finish_rows(chip.astype(jnp.int32)[None], blocks, rows)
    fresh = exchange(fresh_rows, CHIPS).reshape(ROWS, D)
    fresh_other = lax.ppermute(fresh, "core", SWAP)
    fresh_all = in_core_order(core, fresh, fresh_other)

    scores, trios = level_two_scores(fresh, groups_both, counts)
    sums = level_two_sums(scores, exchange(trios, CHIPS), fresh)
    blocks = exchange(sums.reshape(32, 8, WIDE), ("core", *CENT))
    rows = lax.dynamic_slice_in_dim(groups, cent * 8, 8, axis=0)
    new_groups = exchange(finish_groups(blocks, rows), CENT).reshape(128, D)
    return (fresh_all, new_groups)


def solution(mesh):
    split = Mesh(mesh.devices.reshape(2, 8, 2, 4, 4), ("y_hi", "z", "core", "y_lo", "x"))
    return jax.shard_map(
        on_device,
        mesh=split,
        in_specs=(P(DP, None), P(CENT, DP), P(DP, None)),
        out_specs=(P(CENT, None), P(DP, None)),
        check_vma=False,
    )
```

```python
import jax
import jax.numpy as jnp
from jax import lax
from jax.experimental import pallas as pl
from jax.experimental.pallas import tpu as pltpu
from jax.sharding import Mesh, PartitionSpec as P

temper = 20.0
f32, bf16 = jnp.float32, jnp.bfloat16
DP = ("y_hi", "z", "core")
CHIPS = ("y_hi", "z")
CENT = ("y_lo", "x")
SWAP = [(0, 1), (1, 0)]
D = 1024
WIDE = 1152
ROWS = 384
OWN = 24
PACK = 200
FAR = 144
HALF = 192
VMEM = pl.BlockSpec(memory_space=pltpu.VMEM)
SMEM = pl.BlockSpec(memory_space=pltpu.SMEM)
NT = (((1,), (1,)), ((), ()))
NN = (((1,), (0,)), ((), ()))


def params(mib=8):
    return pltpu.CompilerParams(vmem_limit_bytes=mib * 1024 * 1024)


def cost(flops, nbytes, exps=0):
    return pl.CostEstimate(flops=flops, bytes_accessed=nbytes, transcendentals=exps)


def count_row(count):
    high = count.astype(bf16).astype(f32)
    mid = (count - high).astype(bf16).astype(f32)
    low = count - high - mid
    lane = lax.broadcasted_iota(jnp.int32, (OWN, 128), 1)
    row = lax.broadcasted_iota(jnp.int32, (OWN, 128), 0)
    placed = jnp.where(lane == row, high, 0.0)
    placed = jnp.where(lane == row + OWN, mid, placed)
    placed = jnp.where(lane == row + 2 * OWN, low, placed)
    return jnp.sum(placed, axis=0, keepdims=True)


def count_lanes(count):
    n = count.shape[0]
    high = count.astype(bf16).astype(f32)
    mid = (count - high).astype(bf16).astype(f32)
    low = count - high - mid
    lane = lax.broadcasted_iota(jnp.int32, (n, 128), 1)
    wide = jnp.where(lane == 0, high, jnp.where(lane == 1, mid, jnp.where(lane == 2, low, 0.0)))
    return wide.astype(bf16)


def add_up(blocks_ref, n):
    total = blocks_ref[0].astype(f32)
    for i in range(1, n):
        total = total + blocks_ref[i].astype(f32)
    count = jnp.sum(total[:, D:], axis=1, keepdims=True)
    return total[:, :D], count


def scores_kernel(piece_t, points_a, points_b, piece, scores_a, scores_b, pairs, norm):
    @pl.when(pl.program_id(0) == 0)
    def _():
        rows = piece_t[...].T
        piece[...] = rows
        wide = rows.astype(f32)
        norm[...] = jnp.sum(wide * wide, axis=1, keepdims=True)

    found = []
    for points, scores in ((points_a, scores_a), (points_b, scores_b)):
        product = lax.dot_general(piece[...], points[...], NT, preferred_element_type=f32)
        s = (2.0 * product - norm[...]) / temper
        scores[...] = s
        peak = jnp.max(s, axis=0, keepdims=True)
        found += [peak, jnp.sum(jnp.exp(s - peak), axis=0, keepdims=True)]
    block = jnp.concatenate(found, axis=0)
    for i in range(16):
        pairs[i] = block


def level_one_scores(piece_t, points_a, points_b):
    step = 256
    points_spec = pl.BlockSpec((step, D), lambda i: (i, 0))
    scores_spec = pl.BlockSpec((ROWS, step), lambda i: (0, i))
    return pl.pallas_call(
        scores_kernel,
        grid=(1024 // step,),
        in_specs=[pl.BlockSpec((D, ROWS), lambda i: (0, 0)), points_spec, points_spec],
        out_specs=[
            pl.BlockSpec((ROWS, D), lambda i: (0, 0)),
            scores_spec,
            scores_spec,
            pl.BlockSpec((16, 4, step), lambda i: (0, 0, i)),
        ],
        out_shape=[
            jax.ShapeDtypeStruct((ROWS, D), bf16),
            jax.ShapeDtypeStruct((ROWS, 1024), f32),
            jax.ShapeDtypeStruct((ROWS, 1024), f32),
            jax.ShapeDtypeStruct((16, 4, 1024), f32),
        ],
        scratch_shapes=[pltpu.VMEM((ROWS, 1), f32)],
        compiler_params=params(24),
        cost_estimate=cost(2 * ROWS * 2048 * D, 8 << 20, ROWS * 2048),
    )(piece_t, points_a, points_b)


def combine_kernel(pairs, out):
    for row in (0, 2):
        peaks, totals = pairs[:, row, :], pairs[:, row + 1, :]
        peak = jnp.max(peaks, axis=0, keepdims=True)
        out[row : row + 1, :] = peak
        out[row + 1 : row + 2, :] = jnp.sum(
            totals * jnp.exp(peaks - peak), axis=0, keepdims=True
        )


def combine(pairs):
    return pl.pallas_call(
        combine_kernel,
        in_specs=[VMEM],
        out_specs=VMEM,
        out_shape=jax.ShapeDtypeStruct((4, 1024), f32),
        compiler_params=params(),
        cost_estimate=cost(1 << 17, 1 << 18, 1 << 15),
    )(pairs)


def sums_kernel(mine, other, scores_a, scores_b, points_a, points_b, out, total, count):
    @pl.when(pl.program_id(0) == 0)
    def _():
        total[...] = jnp.zeros_like(total)
        count[...] = jnp.zeros_like(count)

    for at, points, scores in ((0, points_a, scores_a), (2, points_b, scores_b)):
        peak_m, total_m = mine[at : at + 1, :], mine[at + 1 : at + 2, :]
        peak_o, total_o = other[2 - at : 3 - at, :], other[3 - at : 4 - at, :]
        peak = jnp.maximum(peak_m, peak_o)
        whole = total_m * jnp.exp(peak_m - peak) + total_o * jnp.exp(peak_o - peak)
        resp = (jnp.exp(scores[...] - peak) * (1.0 / whole)).astype(bf16)
        total[...] += lax.dot_general(resp, points[...], NN, preferred_element_type=f32)
        count[...] += jnp.sum(resp.astype(f32), axis=1, keepdims=True)

    @pl.when(pl.program_id(0) == pl.num_programs(0) - 1)
    def _():
        for b in range(16):
            at = slice(b * OWN, (b + 1) * OWN)
            parts = [total[at, j * 128 : (j + 1) * 128] for j in range(8)]
            tail = jnp.zeros((7, 128), f32)
            out[b] = jnp.concatenate([*parts, count_row(count[at, :]), tail], axis=0).astype(bf16)


def level_one_sums(mine, other, scores_a, scores_b, points_a, points_b):
    step = 512
    pair_spec = pl.BlockSpec((4, step), lambda i: (0, i))
    points_spec = pl.BlockSpec((step, D), lambda i: (i, 0))
    scores_spec = pl.BlockSpec((ROWS, step), lambda i: (0, i))
    return pl.pallas_call(
        sums_kernel,
        grid=(1024 // step,),
        in_specs=[pair_spec, pair_spec, scores_spec, scores_spec, points_spec, points_spec],
        out_specs=pl.BlockSpec((16, PACK, 128), lambda i: (0, 0, 0)),
        out_shape=jax.ShapeDtypeStruct((16, PACK, 128), bf16),
        scratch_shapes=[pltpu.VMEM((ROWS, D), f32), pltpu.VMEM((ROWS, 1), f32)],
        compiler_params=params(24),
        cost_estimate=cost(2 * ROWS * 2048 * D, 8 << 20, ROWS * 2048),
    )(mine, other, scores_a, scores_b, points_a, points_b)


def fresh_kernel(z, blocks, rows, fresh, counts):
    total = blocks[0].astype(f32)
    for i in range(1, 16):
        total = total + blocks[i].astype(f32)
    sums = jnp.concatenate([total[j * OWN : (j + 1) * OWN] for j in range(8)], axis=1)
    lane = lax.broadcasted_iota(jnp.int32, (OWN, 128), 1)
    row = lax.broadcasted_iota(jnp.int32, (OWN, 128), 0)
    part = (lane == row) | (lane == row + OWN) | (lane == row + 2 * OWN)
    count = jnp.sum(jnp.where(part, total[192:193], 0.0), axis=1, keepdims=True)
    new = ((sums + rows[...].astype(f32)) / (count + 1.0)).astype(bf16)
    for i in range(8):
        fresh[i] = new
    lane = lax.broadcasted_iota(jnp.int32, (OWN, 256), 1)
    row = lax.broadcasted_iota(jnp.int32, (OWN, 256), 0)
    placed = jnp.where(lane == row + z[0] * OWN, count, 0.0)
    counts[...] = jnp.sum(placed, axis=0, keepdims=True)


def finish_rows(z, blocks, rows):
    return pl.pallas_call(
        fresh_kernel,
        in_specs=[SMEM, VMEM, VMEM],
        out_specs=[VMEM, VMEM],
        out_shape=[
            jax.ShapeDtypeStruct((8, OWN, D), bf16),
            jax.ShapeDtypeStruct((1, 256), f32),
        ],
        compiler_params=params(),
        cost_estimate=cost(1 << 19, 1 << 20),
    )(z, blocks, rows)


def group_scores_kernel(core, fresh, near, far, counts, scores, trios):
    groups = jnp.concatenate([near[...], far[...]], axis=0)
    wide = groups.astype(f32)
    norm = jnp.sum(wide * wide, axis=1, keepdims=True)
    zero = jnp.zeros((1, HALF), f32)
    blocks = []
    for c in range(2):
        product = lax.dot_general(groups, fresh[c], NT, preferred_element_type=f32)
        s = (2.0 * product - norm) / temper
        scores[c] = s
        peak = jnp.max(s, axis=0, keepdims=True)
        total = jnp.sum(jnp.exp(s - peak), axis=0, keepdims=True)
        count = jnp.where(core[0] == c, counts[:, :HALF], zero)
        blocks += [peak, total, count, zero]
    block = jnp.concatenate(blocks, axis=0)
    for i in range(16):
        trios[i, :, :HALF] = block
        trios[i, :, HALF:] = jnp.zeros((8, 256 - HALF), f32)


def level_two_scores(core, fresh, near, far, counts):
    return pl.pallas_call(
        group_scores_kernel,
        in_specs=[SMEM] + [VMEM] * 4,
        out_specs=[VMEM] * 2,
        out_shape=[
            jax.ShapeDtypeStruct((2, 256, HALF), f32),
            jax.ShapeDtypeStruct((16, 8, 256), f32),
        ],
        compiler_params=params(),
        cost_estimate=cost(2 * ROWS * 256 * D, 2 << 20, ROWS * 256),
    )(core, fresh, near, far, counts)


def exponents_kernel(scores, out, peaks):
    for c in range(2):
        s = scores[c]
        peak = jnp.max(s, axis=0, keepdims=True)
        out[c] = jnp.exp(s - peak)
        peaks[c] = peak


def level_two_exponents(scores):
    return pl.pallas_call(
        exponents_kernel,
        in_specs=[VMEM],
        out_specs=[VMEM] * 2,
        out_shape=[
            jax.ShapeDtypeStruct((2, 256, HALF), f32),
            jax.ShapeDtypeStruct((2, 1, HALF), f32),
        ],
        compiler_params=params(),
        cost_estimate=cost(ROWS * 512, 2 << 20, ROWS * 256),
    )(scores)


def group_sums_kernel(y_hi, expo, here, trios, fresh, out):
    sums, count = jnp.zeros((256, D), f32), jnp.zeros((256, 1), f32)
    for c in range(2):
        at = 4 * c
        peaks, totals = trios[:, at, :], trios[:, at + 1, :]
        peak = jnp.max(peaks, axis=0, keepdims=True)
        whole = jnp.sum(totals * jnp.exp(peaks - peak), axis=0, keepdims=True)
        counts = jnp.sum(trios[:, at + 2, :], axis=0, keepdims=True)
        peak, whole, counts = [v[:, :HALF] for v in (peak, whole, counts)]
        resp = (expo[c] * (jnp.exp(here[c] - peak) / whole)).astype(bf16)
        weighted = (counts * resp.astype(f32)).astype(bf16)
        sums = sums + lax.dot_general(weighted, fresh[c], NN, preferred_element_type=f32)
        count = count + jnp.sum(weighted.astype(f32), axis=1, keepdims=True)
    lanes = count_lanes(count)
    for place, at in ((y_hi[0], 0), (1 - y_hi[0], 128)):
        out[place, :, :D] = sums[at : at + 128].astype(bf16)
        out[place, :, D:] = lanes[at : at + 128]


def level_two_sums(y_hi, expo, here, trios, fresh):
    return pl.pallas_call(
        group_sums_kernel,
        in_specs=[SMEM] + [VMEM] * 4,
        out_specs=VMEM,
        out_shape=jax.ShapeDtypeStruct((2, 128, WIDE), bf16),
        compiler_params=params(),
        cost_estimate=cost(2 * ROWS * 256 * D, 2 << 20, ROWS * 256),
    )(y_hi, expo, here, trios, fresh)


def groups_kernel(blocks, rows, out):
    sums, count = add_up(blocks, 32)
    new = ((sums + rows[...].astype(f32)) / (count + 1.0)).astype(bf16)
    for i in range(16):
        out[i] = new


def finish_groups(blocks, rows):
    return pl.pallas_call(
        groups_kernel,
        in_specs=[VMEM] * 2,
        out_specs=VMEM,
        out_shape=jax.ShapeDtypeStruct((16, 8, D), bf16),
        compiler_params=params(),
        cost_estimate=cost(1 << 19, 1 << 20),
    )(blocks, rows)


def exchange(blocks, axes):
    return lax.all_to_all(blocks, axes, 0, 0)


def ordered(index, mine, other):
    return jnp.where(index == 0, mine, other), jnp.where(index == 0, other, mine)


MIRROR = [(h * 4 + y, (1 - h) * 4 + 3 - y) for h in range(2) for y in range(4)]


def on_device(points, centroids, groups):
    core = lax.axis_index("core")
    y_hi = lax.axis_index("y_hi")
    z = lax.axis_index("z")
    cent = lax.axis_index(CENT)
    core_scalar = core.astype(jnp.int32)[None]
    y_scalar = y_hi.astype(jnp.int32)[None]

    columns = centroids.T
    target = lax.broadcasted_iota(jnp.int32, (32, 1, 1), 0) % 2
    to_send = jnp.where(target == 0, columns[None, :, :ROWS], columns[None, :, ROWS:])
    to_send, points = lax.optimization_barrier((to_send, points))
    piece_t = exchange(to_send, DP).reshape(D, ROWS)
    points_other = lax.ppermute(points, "core", SWAP)

    piece, scores_a, scores_b, pairs = level_one_scores(piece_t, points, points_other)
    mine = combine(exchange(pairs, CENT))
    other = lax.ppermute(mine, "core", SWAP)
    blocks = level_one_sums(mine, other, scores_a, scores_b, points, points_other)
    blocks = exchange(blocks, CHIPS)
    rows = lax.dynamic_slice_in_dim(piece, (y_hi * 8 + z) * OWN, OWN, axis=0)
    fresh_rows, counts = finish_rows(z.astype(jnp.int32)[None], blocks, rows)

    fresh_rows, groups_ready = lax.optimization_barrier((fresh_rows, groups))
    mine = exchange(fresh_rows, "z").reshape(HALF, D)
    groups_far = lax.ppermute(groups_ready, ("y_hi", "y_lo"), MIRROR)
    fresh = lax.all_gather(mine, "core")

    scores, trios = level_two_scores(core_scalar, fresh, groups, groups_far, counts)
    expo, here = level_two_exponents(scores)
    odd = z % 2
    rest = HALF - FAR
    expo, mine = lax.optimization_barrier((expo, mine))
    part = lax.dynamic_slice_in_dim(mine, odd * rest, FAR, axis=0)
    part = lax.ppermute(part, "y_hi", SWAP)
    trios = exchange(trios, ("z", "core"))
    sums = level_two_sums(y_scalar, expo, here, trios, fresh)
    sums, part = lax.optimization_barrier((sums, part))
    lacking = jnp.where(odd == 0, part[:rest], part[FAR - rest :])
    lacking = lax.ppermute(lacking, "z", [(i, i ^ 1) for i in range(8)])
    far_mine = jnp.where(
        odd == 0,
        jnp.concatenate([part, lacking], axis=0),
        jnp.concatenate([lacking, part], axis=0),
    )
    blocks = exchange(sums.reshape(32, 8, WIDE), ("y_hi", *CENT))
    rows = lax.dynamic_slice_in_dim(groups, cent * 8, 8, axis=0)
    new_rows = finish_groups(blocks, rows)
    far_other = lax.ppermute(far_mine, "core", SWAP)
    new_groups = exchange(new_rows, CENT).reshape(128, D)

    far = ordered(core, far_mine, far_other)
    first, second = ordered(y_hi, fresh[0], far[0]), ordered(y_hi, fresh[1], far[1])
    return (jnp.concatenate([*first, *second], axis=0), new_groups)


def solution(mesh):
    split = Mesh(mesh.devices.reshape(2, 8, 2, 4, 4), ("y_hi", "z", "core", "y_lo", "x"))
    return jax.shard_map(
        on_device,
        mesh=split,
        in_specs=(P(DP, None), P(CENT, DP), P(DP, None)),
        out_specs=(P(CENT, None), P(DP, None)),
        check_vma=False,
    )
```

```python
import jax
import jax.numpy as jnp
from jax import lax
from jax.experimental import pallas as pl
from jax.experimental.pallas import tpu as pltpu
from jax.sharding import Mesh, PartitionSpec as P

temper = 20.0
f32, bf16 = jnp.float32, jnp.bfloat16
DP = ("y_hi", "z", "core")
CHIPS = ("y_hi", "z")
CENT = ("y_lo", "x")
SWAP = [(0, 1), (1, 0)]
D = 1024
WIDE = 1152
STEP = 256
ROWS = 384
OWN = 24
PACK = 200
FAR = 144
HALF = 192
VMEM = pl.BlockSpec(memory_space=pltpu.VMEM)
SMEM = pl.BlockSpec(memory_space=pltpu.SMEM)
NT = (((1,), (1,)), ((), ()))
NN = (((1,), (0,)), ((), ()))


def params(mib=8):
    return pltpu.CompilerParams(vmem_limit_bytes=mib * 1024 * 1024)


def cost(flops, nbytes, exps=0):
    return pl.CostEstimate(flops=flops, bytes_accessed=nbytes, transcendentals=exps)


def count_row(count):
    high = count.astype(bf16).astype(f32)
    mid = (count - high).astype(bf16).astype(f32)
    low = count - high - mid
    lane = lax.broadcasted_iota(jnp.int32, (OWN, 128), 1)
    row = lax.broadcasted_iota(jnp.int32, (OWN, 128), 0)
    placed = jnp.where(lane == row, high, 0.0)
    placed = jnp.where(lane == row + OWN, mid, placed)
    placed = jnp.where(lane == row + 2 * OWN, low, placed)
    return jnp.sum(placed, axis=0, keepdims=True)


def count_lanes(count):
    n = count.shape[0]
    high = count.astype(bf16).astype(f32)
    mid = (count - high).astype(bf16).astype(f32)
    low = count - high - mid
    lane = lax.broadcasted_iota(jnp.int32, (n, 128), 1)
    wide = jnp.where(lane == 0, high, jnp.where(lane == 1, mid, jnp.where(lane == 2, low, 0.0)))
    return wide.astype(bf16)


def add_up(blocks_ref, n):
    total = blocks_ref[0].astype(f32)
    for i in range(1, n):
        total = total + blocks_ref[i].astype(f32)
    count = jnp.sum(total[:, D:], axis=1, keepdims=True)
    return total[:, :D], count


def spread_kernel(columns, out):
    for i in range(32):
        out[i] = columns[:, (i % 2) * ROWS : (i % 2 + 1) * ROWS]


def spread_halves(columns):
    return pl.pallas_call(
        spread_kernel,
        in_specs=[VMEM],
        out_specs=VMEM,
        out_shape=jax.ShapeDtypeStruct((32, 32, ROWS), bf16),
        compiler_params=params(),
        cost_estimate=cost(0, 1 << 20),
    )(columns)


def scores_kernel(piece_t, points_a, points_b, piece, scores_a, scores_b, pairs):
    rows = piece_t[...].T
    piece[...] = rows
    wide = rows.astype(f32)
    norm = jnp.sum(wide * wide, axis=1, keepdims=True)
    for i in range(1024 // STEP):
        at = slice(i * STEP, (i + 1) * STEP)
        found = []
        for points, scores in ((points_a, scores_a), (points_b, scores_b)):
            product = lax.dot_general(piece[...], points[at, :], NT, preferred_element_type=f32)
            s = (2.0 * product - norm) * (1.0 / temper)
            scores[:, at] = s
            peak = jnp.max(s, axis=0, keepdims=True)
            found += [peak, jnp.sum(jnp.exp(s - peak), axis=0, keepdims=True)]
        block = jnp.concatenate(found, axis=0)
        for j in range(16):
            pairs[j, :, at] = block


def level_one_scores(piece_t, points_a, points_b):
    return pl.pallas_call(
        scores_kernel,
        in_specs=[VMEM] * 3,
        out_specs=[VMEM] * 4,
        out_shape=[
            jax.ShapeDtypeStruct((ROWS, D), bf16),
            jax.ShapeDtypeStruct((ROWS, 1024), f32),
            jax.ShapeDtypeStruct((ROWS, 1024), f32),
            jax.ShapeDtypeStruct((16, 4, 1024), f32),
        ],
        compiler_params=params(16),
        cost_estimate=cost(2 * ROWS * 2048 * D, 8 << 20, ROWS * 2048),
    )(piece_t, points_a, points_b)


def combine_kernel(pairs, out):
    for row in (0, 2):
        peaks, totals = pairs[:, row, :], pairs[:, row + 1, :]
        peak = jnp.max(peaks, axis=0, keepdims=True)
        out[row : row + 1, :] = peak
        out[row + 1 : row + 2, :] = jnp.sum(
            totals * jnp.exp(peaks - peak), axis=0, keepdims=True
        )


def combine(pairs):
    return pl.pallas_call(
        combine_kernel,
        in_specs=[VMEM],
        out_specs=VMEM,
        out_shape=jax.ShapeDtypeStruct((4, 1024), f32),
        compiler_params=params(),
        cost_estimate=cost(1 << 17, 1 << 18, 1 << 15),
    )(pairs)


def sums_kernel(mine, other, scores_a, scores_b, points_a, points_b, out, resp, total):
    count = jnp.zeros((ROWS, 1), f32)
    for at, scores in ((0, scores_a), (2, scores_b)):
        peak_m, total_m = mine[at : at + 1, :], mine[at + 1 : at + 2, :]
        peak_o, total_o = other[2 - at : 3 - at, :], other[3 - at : 4 - at, :]
        peak = jnp.maximum(peak_m, peak_o)
        whole = total_m * jnp.exp(peak_m - peak) + total_o * jnp.exp(peak_o - peak)
        part = (jnp.exp(scores[...] - peak) * (1.0 / whole)).astype(bf16)
        resp[at // 2] = part
        count = count + jnp.sum(part.astype(f32), axis=1, keepdims=True)
    for j in range(1024 // STEP):
        at = slice(j * STEP, (j + 1) * STEP)
        total[:, at] = lax.dot_general(
            resp[0], points_a[:, at], NN, preferred_element_type=f32
        ) + lax.dot_general(resp[1], points_b[:, at], NN, preferred_element_type=f32)
    for b in range(16):
        at = slice(b * OWN, (b + 1) * OWN)
        parts = [total[at, j * 128 : (j + 1) * 128] for j in range(8)]
        tail = jnp.zeros((7, 128), f32)
        out[b] = jnp.concatenate([*parts, count_row(count[at, :]), tail], axis=0).astype(bf16)


def level_one_sums(mine, other, scores_a, scores_b, points_a, points_b):
    return pl.pallas_call(
        sums_kernel,
        in_specs=[VMEM] * 6,
        out_specs=VMEM,
        out_shape=jax.ShapeDtypeStruct((16, PACK, 128), bf16),
        scratch_shapes=[pltpu.VMEM((2, ROWS, 1024), bf16), pltpu.VMEM((ROWS, D), f32)],
        compiler_params=params(24),
        cost_estimate=cost(2 * ROWS * 2048 * D, 8 << 20, ROWS * 2048),
    )(mine, other, scores_a, scores_b, points_a, points_b)


def fresh_kernel(z, blocks, rows, fresh, counts):
    total = blocks[0].astype(f32)
    for i in range(1, 16):
        total = total + blocks[i].astype(f32)
    sums = jnp.concatenate([total[j * OWN : (j + 1) * OWN] for j in range(8)], axis=1)
    lane = lax.broadcasted_iota(jnp.int32, (OWN, 128), 1)
    row = lax.broadcasted_iota(jnp.int32, (OWN, 128), 0)
    part = (lane == row) | (lane == row + OWN) | (lane == row + 2 * OWN)
    count = jnp.sum(jnp.where(part, total[192:193], 0.0), axis=1, keepdims=True)
    new = ((sums + rows[...].astype(f32)) / (count + 1.0)).astype(bf16)
    for i in range(8):
        fresh[i] = new
    lane = lax.broadcasted_iota(jnp.int32, (OWN, 256), 1)
    row = lax.broadcasted_iota(jnp.int32, (OWN, 256), 0)
    placed = jnp.where(lane == row + z[0] * OWN, count, 0.0)
    counts[...] = jnp.sum(placed, axis=0, keepdims=True)


def finish_rows(z, blocks, rows):
    return pl.pallas_call(
        fresh_kernel,
        in_specs=[SMEM, VMEM, VMEM],
        out_specs=[VMEM, VMEM],
        out_shape=[
            jax.ShapeDtypeStruct((8, OWN, D), bf16),
            jax.ShapeDtypeStruct((1, 256), f32),
        ],
        compiler_params=params(),
        cost_estimate=cost(1 << 19, 1 << 20),
    )(z, blocks, rows)


def group_scores_kernel(core, fresh, near, far, counts, scores, trios):
    groups = jnp.concatenate([near[...], far[...]], axis=0)
    wide = groups.astype(f32)
    norm = jnp.sum(wide * wide, axis=1, keepdims=True)
    zero = jnp.zeros((1, HALF), f32)
    blocks = []
    for c in range(2):
        product = lax.dot_general(groups, fresh[c], NT, preferred_element_type=f32)
        s = (2.0 * product - norm) / temper
        scores[c] = s
        peak = jnp.max(s, axis=0, keepdims=True)
        total = jnp.sum(jnp.exp(s - peak), axis=0, keepdims=True)
        count = jnp.where(core[0] == c, counts[:, :HALF], zero)
        blocks += [peak, total, count, zero]
    block = jnp.concatenate(blocks, axis=0)
    for i in range(16):
        trios[i, :, :HALF] = block
        trios[i, :, HALF:] = jnp.zeros((8, 256 - HALF), f32)


def level_two_scores(core, fresh, near, far, counts):
    return pl.pallas_call(
        group_scores_kernel,
        in_specs=[SMEM] + [VMEM] * 4,
        out_specs=[VMEM] * 2,
        out_shape=[
            jax.ShapeDtypeStruct((2, 256, HALF), f32),
            jax.ShapeDtypeStruct((16, 8, 256), f32),
        ],
        compiler_params=params(),
        cost_estimate=cost(2 * ROWS * 256 * D, 2 << 20, ROWS * 256),
    )(core, fresh, near, far, counts)


def exponents_kernel(scores, out, peaks):
    for c in range(2):
        s = scores[c]
        peak = jnp.max(s, axis=0, keepdims=True)
        out[c] = jnp.exp(s - peak)
        peaks[c] = peak


def level_two_exponents(scores):
    return pl.pallas_call(
        exponents_kernel,
        in_specs=[VMEM],
        out_specs=[VMEM] * 2,
        out_shape=[
            jax.ShapeDtypeStruct((2, 256, HALF), f32),
            jax.ShapeDtypeStruct((2, 1, HALF), f32),
        ],
        compiler_params=params(),
        cost_estimate=cost(ROWS * 512, 2 << 20, ROWS * 256),
    )(scores)


def group_sums_kernel(y_hi, expo, here, trios, fresh, out):
    sums, count = jnp.zeros((256, D), f32), jnp.zeros((256, 1), f32)
    for c in range(2):
        at = 4 * c
        peaks, totals = trios[:, at, :], trios[:, at + 1, :]
        peak = jnp.max(peaks, axis=0, keepdims=True)
        whole = jnp.sum(totals * jnp.exp(peaks - peak), axis=0, keepdims=True)
        counts = jnp.sum(trios[:, at + 2, :], axis=0, keepdims=True)
        peak, whole, counts = [v[:, :HALF] for v in (peak, whole, counts)]
        resp = (expo[c] * (jnp.exp(here[c] - peak) / whole)).astype(bf16)
        weighted = (counts * resp.astype(f32)).astype(bf16)
        sums = sums + lax.dot_general(weighted, fresh[c], NN, preferred_element_type=f32)
        count = count + jnp.sum(weighted.astype(f32), axis=1, keepdims=True)
    lanes = count_lanes(count)
    for place, at in ((y_hi[0], 0), (1 - y_hi[0], 128)):
        out[place, :, :D] = sums[at : at + 128].astype(bf16)
        out[place, :, D:] = lanes[at : at + 128]


def level_two_sums(y_hi, expo, here, trios, fresh):
    return pl.pallas_call(
        group_sums_kernel,
        in_specs=[SMEM] + [VMEM] * 4,
        out_specs=VMEM,
        out_shape=jax.ShapeDtypeStruct((2, 128, WIDE), bf16),
        compiler_params=params(),
        cost_estimate=cost(2 * ROWS * 256 * D, 2 << 20, ROWS * 256),
    )(y_hi, expo, here, trios, fresh)


def groups_kernel(blocks, rows, out):
    sums, count = add_up(blocks, 32)
    new = ((sums + rows[...].astype(f32)) / (count + 1.0)).astype(bf16)
    for i in range(16):
        out[i] = new


def finish_groups(blocks, rows):
    return pl.pallas_call(
        groups_kernel,
        in_specs=[VMEM] * 2,
        out_specs=VMEM,
        out_shape=jax.ShapeDtypeStruct((16, 8, D), bf16),
        compiler_params=params(),
        cost_estimate=cost(1 << 19, 1 << 20),
    )(blocks, rows)


def exchange(blocks, axes):
    return lax.all_to_all(blocks, axes, 0, 0)


def ordered(index, mine, other):
    return jnp.where(index == 0, mine, other), jnp.where(index == 0, other, mine)


MIRROR = [(h * 4 + y, (1 - h) * 4 + 3 - y) for h in range(2) for y in range(4)]


def on_device(points, centroids, groups):
    core = lax.axis_index("core")
    y_hi = lax.axis_index("y_hi")
    z = lax.axis_index("z")
    cent = lax.axis_index(CENT)
    core_scalar = core.astype(jnp.int32)[None]
    y_scalar = y_hi.astype(jnp.int32)[None]

    to_send = spread_halves(centroids.T)
    to_send, points = lax.optimization_barrier((to_send, points))
    piece_t = exchange(to_send, DP).reshape(D, ROWS)
    points_other = lax.ppermute(points, "core", SWAP)

    piece, scores_a, scores_b, pairs = level_one_scores(piece_t, points, points_other)
    mine = combine(exchange(pairs, CENT))
    other = lax.ppermute(mine, "core", SWAP)
    blocks = level_one_sums(mine, other, scores_a, scores_b, points, points_other)
    blocks = exchange(blocks, CHIPS)
    rows = lax.dynamic_slice_in_dim(piece, (y_hi * 8 + z) * OWN, OWN, axis=0)
    fresh_rows, counts = finish_rows(z.astype(jnp.int32)[None], blocks, rows)

    fresh_rows, groups_ready = lax.optimization_barrier((fresh_rows, groups))
    mine = exchange(fresh_rows, "z").reshape(HALF, D)
    groups_far = lax.ppermute(groups_ready, ("y_hi", "y_lo"), MIRROR)
    fresh = lax.all_gather(mine, "core")

    scores, trios = level_two_scores(core_scalar, fresh, groups, groups_far, counts)
    expo, here = level_two_exponents(scores)
    odd = z % 2
    rest = HALF - FAR
    expo, mine = lax.optimization_barrier((expo, mine))
    part = lax.dynamic_slice_in_dim(mine, odd * rest, FAR, axis=0)
    part = lax.ppermute(part, "y_hi", SWAP)
    trios = exchange(trios, ("z", "core"))
    sums = level_two_sums(y_scalar, expo, here, trios, fresh)
    sums, part = lax.optimization_barrier((sums, part))
    lacking = jnp.where(odd == 0, part[:rest], part[FAR - rest :])
    lacking = lax.ppermute(lacking, "z", [(i, i ^ 1) for i in range(8)])
    far_mine = jnp.where(
        odd == 0,
        jnp.concatenate([part, lacking], axis=0),
        jnp.concatenate([lacking, part], axis=0),
    )
    blocks = exchange(sums.reshape(32, 8, WIDE), ("y_hi", *CENT))
    rows = lax.dynamic_slice_in_dim(groups, cent * 8, 8, axis=0)
    new_rows = finish_groups(blocks, rows)
    far_other = lax.ppermute(far_mine, "core", SWAP)
    new_groups = exchange(new_rows, CENT).reshape(128, D)

    far = ordered(core, far_mine, far_other)
    first, second = ordered(y_hi, fresh[0], far[0]), ordered(y_hi, fresh[1], far[1])
    return (jnp.concatenate([*first, *second], axis=0), new_groups)


def solution(mesh):
    split = Mesh(mesh.devices.reshape(2, 8, 2, 4, 4), ("y_hi", "z", "core", "y_lo", "x"))
    return jax.shard_map(
        on_device,
        mesh=split,
        in_specs=(P(DP, None), P(CENT, DP), P(DP, None)),
        out_specs=(P(CENT, None), P(DP, None)),
        check_vma=False,
    )
```

```python
import jax
import jax.numpy as jnp
from jax import lax
from jax.experimental import pallas as pl
from jax.experimental.pallas import tpu as pltpu
from jax.sharding import Mesh, PartitionSpec as P

temper = 20.0
f32, bf16 = jnp.float32, jnp.bfloat16
DP = ("y_hi", "z", "core")
CHIPS = ("y_hi", "z")
CENT = ("y_lo", "x")
NEAR = ("x", "y_lo")
SWAP = [(0, 1), (1, 0)]
D = 1024
WIDE = 1152
STEP = 256
ROWS = 384
OWN = 24
PACK = 200
FAR = 144
HALF = 192
VMEM = pl.BlockSpec(memory_space=pltpu.VMEM)
SMEM = pl.BlockSpec(memory_space=pltpu.SMEM)
NT = (((1,), (1,)), ((), ()))
NN = (((1,), (0,)), ((), ()))


def params(mib=8):
    return pltpu.CompilerParams(vmem_limit_bytes=mib * 1024 * 1024)


def cost(flops, nbytes, exps=0):
    return pl.CostEstimate(flops=flops, bytes_accessed=nbytes, transcendentals=exps)


def count_row(count):
    high = count.astype(bf16).astype(f32)
    mid = (count - high).astype(bf16).astype(f32)
    low = count - high - mid
    lane = lax.broadcasted_iota(jnp.int32, (OWN, 128), 1)
    row = lax.broadcasted_iota(jnp.int32, (OWN, 128), 0)
    placed = jnp.where(lane == row, high, 0.0)
    placed = jnp.where(lane == row + OWN, mid, placed)
    placed = jnp.where(lane == row + 2 * OWN, low, placed)
    return jnp.sum(placed, axis=0, keepdims=True)


def count_lanes(count):
    n = count.shape[0]
    high = count.astype(bf16).astype(f32)
    mid = (count - high).astype(bf16).astype(f32)
    low = count - high - mid
    lane = lax.broadcasted_iota(jnp.int32, (n, 128), 1)
    wide = jnp.where(lane == 0, high, jnp.where(lane == 1, mid, jnp.where(lane == 2, low, 0.0)))
    return wide.astype(bf16)


def add_up(blocks_ref, n):
    total = blocks_ref[0].astype(f32)
    for i in range(1, n):
        total = total + blocks_ref[i].astype(f32)
    count = jnp.sum(total[:, D:], axis=1, keepdims=True)
    return total[:, :D], count


def spread_kernel(columns, out):
    for i in range(32):
        out[i] = columns[:, (i % 2) * ROWS : (i % 2 + 1) * ROWS]


def spread_halves(columns):
    return pl.pallas_call(
        spread_kernel,
        in_specs=[VMEM],
        out_specs=VMEM,
        out_shape=jax.ShapeDtypeStruct((32, 32, ROWS), bf16),
        compiler_params=params(),
        cost_estimate=cost(0, 1 << 20),
    )(columns)


def scores_kernel(piece_t, points_a, points_b, piece, scores_a, scores_b, pairs):
    rows = piece_t[...].T
    piece[...] = rows
    wide = rows.astype(f32)
    norm = jnp.sum(wide * wide, axis=1, keepdims=True)
    for i in range(1024 // STEP):
        at = slice(i * STEP, (i + 1) * STEP)
        found = []
        for points, scores in ((points_a, scores_a), (points_b, scores_b)):
            product = lax.dot_general(piece[...], points[at, :], NT, preferred_element_type=f32)
            s = (2.0 * product - norm) * (1.0 / temper)
            scores[:, at] = s
            peak = jnp.max(s, axis=0, keepdims=True)
            found += [peak, jnp.sum(jnp.exp(s - peak), axis=0, keepdims=True)]
        block = jnp.concatenate(found, axis=0)
        for j in range(16):
            pairs[j, :, at] = block


def level_one_scores(piece_t, points_a, points_b):
    return pl.pallas_call(
        scores_kernel,
        in_specs=[VMEM] * 3,
        out_specs=[VMEM] * 4,
        out_shape=[
            jax.ShapeDtypeStruct((ROWS, D), bf16),
            jax.ShapeDtypeStruct((ROWS, 1024), f32),
            jax.ShapeDtypeStruct((ROWS, 1024), f32),
            jax.ShapeDtypeStruct((16, 4, 1024), f32),
        ],
        compiler_params=params(16),
        cost_estimate=cost(2 * ROWS * 2048 * D, 8 << 20, ROWS * 2048),
    )(piece_t, points_a, points_b)


def combine_kernel(pairs, out):
    for row in (0, 2):
        peaks, totals = pairs[:, row, :], pairs[:, row + 1, :]
        peak = jnp.max(peaks, axis=0, keepdims=True)
        out[row : row + 1, :] = peak
        out[row + 1 : row + 2, :] = jnp.sum(
            totals * jnp.exp(peaks - peak), axis=0, keepdims=True
        )


def combine(pairs):
    return pl.pallas_call(
        combine_kernel,
        in_specs=[VMEM],
        out_specs=VMEM,
        out_shape=jax.ShapeDtypeStruct((4, 1024), f32),
        compiler_params=params(),
        cost_estimate=cost(1 << 17, 1 << 18, 1 << 15),
    )(pairs)


def sums_kernel(mine, other, scores_a, scores_b, points_a, points_b, out, resp, total):
    count = jnp.zeros((ROWS, 1), f32)
    for at, scores in ((0, scores_a), (2, scores_b)):
        peak_m, total_m = mine[at : at + 1, :], mine[at + 1 : at + 2, :]
        peak_o, total_o = other[2 - at : 3 - at, :], other[3 - at : 4 - at, :]
        peak = jnp.maximum(peak_m, peak_o)
        whole = total_m * jnp.exp(peak_m - peak) + total_o * jnp.exp(peak_o - peak)
        part = (jnp.exp(scores[...] - peak) * (1.0 / whole)).astype(bf16)
        resp[at // 2] = part
        count = count + jnp.sum(part.astype(f32), axis=1, keepdims=True)
    for j in range(1024 // STEP):
        at = slice(j * STEP, (j + 1) * STEP)
        total[:, at] = lax.dot_general(
            resp[0], points_a[:, at], NN, preferred_element_type=f32
        ) + lax.dot_general(resp[1], points_b[:, at], NN, preferred_element_type=f32)
    for b in range(16):
        at = slice(b * OWN, (b + 1) * OWN)
        parts = [total[at, j * 128 : (j + 1) * 128] for j in range(8)]
        tail = jnp.zeros((7, 128), f32)
        out[b] = jnp.concatenate([*parts, count_row(count[at, :]), tail], axis=0).astype(bf16)


def level_one_sums(mine, other, scores_a, scores_b, points_a, points_b):
    return pl.pallas_call(
        sums_kernel,
        in_specs=[VMEM] * 6,
        out_specs=VMEM,
        out_shape=jax.ShapeDtypeStruct((16, PACK, 128), bf16),
        scratch_shapes=[pltpu.VMEM((2, ROWS, 1024), bf16), pltpu.VMEM((ROWS, D), f32)],
        compiler_params=params(24),
        cost_estimate=cost(2 * ROWS * 2048 * D, 8 << 20, ROWS * 2048),
    )(mine, other, scores_a, scores_b, points_a, points_b)


def fresh_kernel(z, blocks, rows, fresh, counts):
    total = blocks[0].astype(f32)
    for i in range(1, 16):
        total = total + blocks[i].astype(f32)
    sums = jnp.concatenate([total[j * OWN : (j + 1) * OWN] for j in range(8)], axis=1)
    lane = lax.broadcasted_iota(jnp.int32, (OWN, 128), 1)
    row = lax.broadcasted_iota(jnp.int32, (OWN, 128), 0)
    part = (lane == row) | (lane == row + OWN) | (lane == row + 2 * OWN)
    count = jnp.sum(jnp.where(part, total[192:193], 0.0), axis=1, keepdims=True)
    new = ((sums + rows[...].astype(f32)) / (count + 1.0)).astype(bf16)
    for i in range(8):
        fresh[i] = new
    lane = lax.broadcasted_iota(jnp.int32, (OWN, 256), 1)
    row = lax.broadcasted_iota(jnp.int32, (OWN, 256), 0)
    placed = jnp.where(lane == row + z[0] * OWN, count, 0.0)
    counts[...] = jnp.sum(placed, axis=0, keepdims=True)


def finish_rows(z, blocks, rows):
    return pl.pallas_call(
        fresh_kernel,
        in_specs=[SMEM, VMEM, VMEM],
        out_specs=[VMEM, VMEM],
        out_shape=[
            jax.ShapeDtypeStruct((8, OWN, D), bf16),
            jax.ShapeDtypeStruct((1, 256), f32),
        ],
        compiler_params=params(),
        cost_estimate=cost(1 << 19, 1 << 20),
    )(z, blocks, rows)


def group_scores_kernel(core, fresh, near, far, counts, scores, trios):
    groups = jnp.concatenate([near[...], far[...]], axis=0)
    wide = groups.astype(f32)
    norm = jnp.sum(wide * wide, axis=1, keepdims=True)
    zero = jnp.zeros((1, HALF), f32)
    blocks = []
    for c in range(2):
        product = lax.dot_general(groups, fresh[c], NT, preferred_element_type=f32)
        s = (2.0 * product - norm) / temper
        scores[c] = s
        peak = jnp.max(s, axis=0, keepdims=True)
        total = jnp.sum(jnp.exp(s - peak), axis=0, keepdims=True)
        count = jnp.where(core[0] == c, counts[:, :HALF], zero)
        blocks += [peak, total, count, zero]
    block = jnp.concatenate(blocks, axis=0)
    for i in range(16):
        trios[i, :, :HALF] = block
        trios[i, :, HALF:] = jnp.zeros((8, 256 - HALF), f32)


def level_two_scores(core, fresh, near, far, counts):
    return pl.pallas_call(
        group_scores_kernel,
        in_specs=[SMEM] + [VMEM] * 4,
        out_specs=[VMEM] * 2,
        out_shape=[
            jax.ShapeDtypeStruct((2, 256, HALF), f32),
            jax.ShapeDtypeStruct((16, 8, 256), f32),
        ],
        compiler_params=params(),
        cost_estimate=cost(2 * ROWS * 256 * D, 2 << 20, ROWS * 256),
    )(core, fresh, near, far, counts)


def exponents_kernel(scores, out, peaks):
    for c in range(2):
        s = scores[c]
        peak = jnp.max(s, axis=0, keepdims=True)
        out[c] = jnp.exp(s - peak)
        peaks[c] = peak


def level_two_exponents(scores):
    return pl.pallas_call(
        exponents_kernel,
        in_specs=[VMEM],
        out_specs=[VMEM] * 2,
        out_shape=[
            jax.ShapeDtypeStruct((2, 256, HALF), f32),
            jax.ShapeDtypeStruct((2, 1, HALF), f32),
        ],
        compiler_params=params(),
        cost_estimate=cost(ROWS * 512, 2 << 20, ROWS * 256),
    )(scores)


def group_sums_kernel(y_hi, expo, here, trios, fresh, out):
    sums, count = jnp.zeros((256, D), f32), jnp.zeros((256, 1), f32)
    for c in range(2):
        at = 4 * c
        peaks, totals = trios[:, at, :], trios[:, at + 1, :]
        peak = jnp.max(peaks, axis=0, keepdims=True)
        whole = jnp.sum(totals * jnp.exp(peaks - peak), axis=0, keepdims=True)
        counts = jnp.sum(trios[:, at + 2, :], axis=0, keepdims=True)
        peak, whole, counts = [v[:, :HALF] for v in (peak, whole, counts)]
        resp = (expo[c] * (jnp.exp(here[c] - peak) / whole)).astype(bf16)
        weighted = (counts * resp.astype(f32)).astype(bf16)
        sums = sums + lax.dot_general(weighted, fresh[c], NN, preferred_element_type=f32)
        count = count + jnp.sum(weighted.astype(f32), axis=1, keepdims=True)
    lanes = count_lanes(count)
    for place, at in ((y_hi[0], 0), (1 - y_hi[0], 128)):
        for i in range(16):
            block = slice(at + i * 8, at + i * 8 + 8)
            out[i, place, :, :D] = sums[block].astype(bf16)
            out[i, place, :, D:] = lanes[block]


def level_two_sums(y_hi, expo, here, trios, fresh):
    return pl.pallas_call(
        group_sums_kernel,
        in_specs=[SMEM] + [VMEM] * 4,
        out_specs=VMEM,
        out_shape=jax.ShapeDtypeStruct((16, 2, 8, WIDE), bf16),
        compiler_params=params(),
        cost_estimate=cost(2 * ROWS * 256 * D, 2 << 20, ROWS * 256),
    )(y_hi, expo, here, trios, fresh)


def groups_kernel(blocks, rows, out):
    sums, count = add_up(blocks, 32)
    new = ((sums + rows[...].astype(f32)) / (count + 1.0)).astype(bf16)
    for i in range(16):
        out[i] = new


def finish_groups(blocks, rows):
    return pl.pallas_call(
        groups_kernel,
        in_specs=[VMEM] * 2,
        out_specs=VMEM,
        out_shape=jax.ShapeDtypeStruct((16, 8, D), bf16),
        compiler_params=params(),
        cost_estimate=cost(1 << 19, 1 << 20),
    )(blocks, rows)


def exchange(blocks, axes):
    return lax.all_to_all(blocks, axes, 0, 0)


def ordered(index, mine, other):
    return jnp.where(index == 0, mine, other), jnp.where(index == 0, other, mine)


MIRROR = [(h * 4 + y, (1 - h) * 4 + 3 - y) for h in range(2) for y in range(4)]


def on_device(points, centroids, groups):
    core = lax.axis_index("core")
    y_hi = lax.axis_index("y_hi")
    z = lax.axis_index("z")
    cent = lax.axis_index(NEAR)
    core_scalar = core.astype(jnp.int32)[None]
    y_scalar = y_hi.astype(jnp.int32)[None]

    to_send = spread_halves(centroids.T)
    to_send, points = lax.optimization_barrier((to_send, points))
    piece_t = exchange(to_send, DP).reshape(D, ROWS)
    points_other = lax.ppermute(points, "core", SWAP)

    piece, scores_a, scores_b, pairs = level_one_scores(piece_t, points, points_other)
    mine = combine(exchange(pairs, NEAR))
    other = lax.ppermute(mine, "core", SWAP)
    blocks = level_one_sums(mine, other, scores_a, scores_b, points, points_other)
    blocks = exchange(blocks, CHIPS)
    rows = lax.dynamic_slice_in_dim(piece, (y_hi * 8 + z) * OWN, OWN, axis=0)
    fresh_rows, counts = finish_rows(z.astype(jnp.int32)[None], blocks, rows)

    fresh_rows, groups_ready = lax.optimization_barrier((fresh_rows, groups))
    mine = exchange(fresh_rows, "z").reshape(HALF, D)
    groups_far = lax.ppermute(groups_ready, ("y_hi", "y_lo"), MIRROR)
    fresh = lax.all_gather(mine, "core")

    scores, trios = level_two_scores(core_scalar, fresh, groups, groups_far, counts)
    expo, here = level_two_exponents(scores)
    odd = z % 2
    rest = HALF - FAR
    expo, mine = lax.optimization_barrier((expo, mine))
    part = lax.dynamic_slice_in_dim(mine, odd * rest, FAR, axis=0)
    part = lax.ppermute(part, "y_hi", SWAP)
    trios = exchange(trios, ("core", "z"))
    sums = level_two_sums(y_scalar, expo, here, trios, fresh)
    sums, part = lax.optimization_barrier((sums, part))
    lacking = jnp.where(odd == 0, part[:rest], part[FAR - rest :])
    lacking = lax.ppermute(lacking, "z", [(i, i ^ 1) for i in range(8)])
    far_mine = jnp.where(
        odd == 0,
        jnp.concatenate([part, lacking], axis=0),
        jnp.concatenate([lacking, part], axis=0),
    )
    blocks = exchange(sums.reshape(32, 8, WIDE), (*NEAR, "y_hi"))
    rows = lax.dynamic_slice_in_dim(groups, cent * 8, 8, axis=0)
    new_rows = finish_groups(blocks, rows)
    far_other = lax.ppermute(far_mine, "core", SWAP)
    new_groups = exchange(new_rows, NEAR).reshape(128, D)

    far = ordered(core, far_mine, far_other)
    first, second = ordered(y_hi, fresh[0], far[0]), ordered(y_hi, fresh[1], far[1])
    return (jnp.concatenate([*first, *second], axis=0), new_groups)


def solution(mesh):
    split = Mesh(mesh.devices.reshape(2, 8, 2, 4, 4), ("y_hi", "z", "core", "y_lo", "x"))
    return jax.shard_map(
        on_device,
        mesh=split,
        in_specs=(P(DP, None), P(CENT, DP), P(DP, None)),
        out_specs=(P(CENT, None), P(DP, None)),
        check_vma=False,
    )
```

```python
import jax
import jax.numpy as jnp
from jax import lax
from jax.experimental import pallas as pl
from jax.experimental.pallas import tpu as pltpu
from jax.sharding import Mesh, PartitionSpec as P

temper = 20.0
f32, bf16 = jnp.float32, jnp.bfloat16
DP = ("y_hi", "z", "core")
CHIPS = ("y_hi", "z")
CENT = ("y_lo", "x")
NEAR = ("x", "y_lo")
SWAP = [(0, 1), (1, 0)]
D = 1024
WIDE = 1152
STEP = 256
ROWS = 384
OWN = 24
PACK = 200
FAR = 144
HALF = 192
VMEM = pl.BlockSpec(memory_space=pltpu.VMEM)
SMEM = pl.BlockSpec(memory_space=pltpu.SMEM)
NT = (((1,), (1,)), ((), ()))
NN = (((1,), (0,)), ((), ()))


def params(mib=8):
    return pltpu.CompilerParams(vmem_limit_bytes=mib * 1024 * 1024)


def cost(flops, nbytes, exps=0):
    return pl.CostEstimate(flops=flops, bytes_accessed=nbytes, transcendentals=exps)


def count_row(count):
    high = count.astype(bf16).astype(f32)
    mid = (count - high).astype(bf16).astype(f32)
    low = count - high - mid
    lane = lax.broadcasted_iota(jnp.int32, (OWN, 128), 1)
    row = lax.broadcasted_iota(jnp.int32, (OWN, 128), 0)
    placed = jnp.where(lane == row, high, 0.0)
    placed = jnp.where(lane == row + OWN, mid, placed)
    placed = jnp.where(lane == row + 2 * OWN, low, placed)
    return jnp.sum(placed, axis=0, keepdims=True)


def count_lanes(count):
    n = count.shape[0]
    high = count.astype(bf16).astype(f32)
    mid = (count - high).astype(bf16).astype(f32)
    low = count - high - mid
    lane = lax.broadcasted_iota(jnp.int32, (n, 128), 1)
    wide = jnp.where(lane == 0, high, jnp.where(lane == 1, mid, jnp.where(lane == 2, low, 0.0)))
    return wide.astype(bf16)


def add_up(blocks_ref, n):
    total = blocks_ref[0].astype(f32)
    for i in range(1, n):
        total = total + blocks_ref[i].astype(f32)
    count = jnp.sum(total[:, D:], axis=1, keepdims=True)
    return total[:, :D], count


def spread_kernel(columns, out):
    for i in range(32):
        out[i] = columns[:, (i % 2) * ROWS : (i % 2 + 1) * ROWS]


def spread_halves(columns):
    return pl.pallas_call(
        spread_kernel,
        in_specs=[VMEM],
        out_specs=VMEM,
        out_shape=jax.ShapeDtypeStruct((32, 32, ROWS), bf16),
        compiler_params=params(),
        cost_estimate=cost(0, 1 << 20),
    )(columns)


def scores_kernel(piece_t, points_a, points_b, piece, scores_a, scores_b, pairs):
    rows = piece_t[...].T
    piece[...] = rows
    wide = rows.astype(f32)
    norm = jnp.sum(wide * wide, axis=1, keepdims=True)
    for i in range(1024 // STEP):
        at = slice(i * STEP, (i + 1) * STEP)
        found = []
        for points, scores in ((points_a, scores_a), (points_b, scores_b)):
            product = lax.dot_general(piece[...], points[at, :], NT, preferred_element_type=f32)
            s = (2.0 * product - norm) * (1.0 / temper)
            scores[:, at] = s
            peak = jnp.max(s, axis=0, keepdims=True)
            found += [peak, jnp.sum(jnp.exp(s - peak), axis=0, keepdims=True)]
        block = jnp.concatenate(found, axis=0)
        for j in range(16):
            pairs[j, :, at] = block


def level_one_scores(piece_t, points_a, points_b):
    return pl.pallas_call(
        scores_kernel,
        in_specs=[VMEM] * 3,
        out_specs=[VMEM] * 4,
        out_shape=[
            jax.ShapeDtypeStruct((ROWS, D), bf16),
            jax.ShapeDtypeStruct((ROWS, 1024), f32),
            jax.ShapeDtypeStruct((ROWS, 1024), f32),
            jax.ShapeDtypeStruct((16, 4, 1024), f32),
        ],
        compiler_params=params(16),
        cost_estimate=cost(2 * ROWS * 2048 * D, 8 << 20, ROWS * 2048),
    )(piece_t, points_a, points_b)


def combine_kernel(pairs, out):
    for row in (0, 2):
        peaks, totals = pairs[:, row, :], pairs[:, row + 1, :]
        peak = jnp.max(peaks, axis=0, keepdims=True)
        out[row : row + 1, :] = peak
        out[row + 1 : row + 2, :] = jnp.sum(
            totals * jnp.exp(peaks - peak), axis=0, keepdims=True
        )


def combine(pairs):
    return pl.pallas_call(
        combine_kernel,
        in_specs=[VMEM],
        out_specs=VMEM,
        out_shape=jax.ShapeDtypeStruct((4, 1024), f32),
        compiler_params=params(),
        cost_estimate=cost(1 << 17, 1 << 18, 1 << 15),
    )(pairs)


def sums_kernel(mine, other, scores_a, scores_b, points_a, points_b, out, resp, total):
    count = jnp.zeros((ROWS, 1), f32)
    for place, scores, points in ((0, scores_a, points_a), (1, scores_b, points_b)):
        at = 2 * place
        peak_m, total_m = mine[at : at + 1, :], mine[at + 1 : at + 2, :]
        peak_o, total_o = other[2 - at : 3 - at, :], other[3 - at : 4 - at, :]
        peak = jnp.maximum(peak_m, peak_o)
        whole = total_m * jnp.exp(peak_m - peak) + total_o * jnp.exp(peak_o - peak)
        part = (jnp.exp(scores[...] - peak) * (1.0 / whole)).astype(bf16)
        resp[place] = part
        count = count + jnp.sum(part.astype(f32), axis=1, keepdims=True)
        for j in range(1024 // STEP):
            cols = slice(j * STEP, (j + 1) * STEP)
            sums = lax.dot_general(
                resp[place], points[:, cols], NN, preferred_element_type=f32
            )
            total[:, cols] = total[:, cols] + sums if place else sums
    for b in range(16):
        at = slice(b * OWN, (b + 1) * OWN)
        parts = [total[at, j * 128 : (j + 1) * 128] for j in range(8)]
        tail = jnp.zeros((7, 128), f32)
        out[b] = jnp.concatenate([*parts, count_row(count[at, :]), tail], axis=0).astype(bf16)


def level_one_sums(mine, other, scores_a, scores_b, points_a, points_b):
    return pl.pallas_call(
        sums_kernel,
        in_specs=[VMEM] * 6,
        out_specs=VMEM,
        out_shape=jax.ShapeDtypeStruct((16, PACK, 128), bf16),
        scratch_shapes=[pltpu.VMEM((2, ROWS, 1024), bf16), pltpu.VMEM((ROWS, D), f32)],
        compiler_params=params(24),
        cost_estimate=cost(2 * ROWS * 2048 * D, 8 << 20, ROWS * 2048),
    )(mine, other, scores_a, scores_b, points_a, points_b)


def fresh_kernel(z, blocks, rows, fresh, counts):
    total = blocks[0].astype(f32)
    for i in range(1, 16):
        total = total + blocks[i].astype(f32)
    sums = jnp.concatenate([total[j * OWN : (j + 1) * OWN] for j in range(8)], axis=1)
    lane = lax.broadcasted_iota(jnp.int32, (OWN, 128), 1)
    row = lax.broadcasted_iota(jnp.int32, (OWN, 128), 0)
    part = (lane == row) | (lane == row + OWN) | (lane == row + 2 * OWN)
    count = jnp.sum(jnp.where(part, total[192:193], 0.0), axis=1, keepdims=True)
    new = ((sums + rows[...].astype(f32)) / (count + 1.0)).astype(bf16)
    for i in range(8):
        fresh[i] = new
    lane = lax.broadcasted_iota(jnp.int32, (OWN, 256), 1)
    row = lax.broadcasted_iota(jnp.int32, (OWN, 256), 0)
    placed = jnp.where(lane == row + z[0] * OWN, count, 0.0)
    counts[...] = jnp.sum(placed, axis=0, keepdims=True)


def finish_rows(z, blocks, rows):
    return pl.pallas_call(
        fresh_kernel,
        in_specs=[SMEM, VMEM, VMEM],
        out_specs=[VMEM, VMEM],
        out_shape=[
            jax.ShapeDtypeStruct((8, OWN, D), bf16),
            jax.ShapeDtypeStruct((1, 256), f32),
        ],
        compiler_params=params(),
        cost_estimate=cost(1 << 19, 1 << 20),
    )(z, blocks, rows)


def group_scores_kernel(core, fresh, near, far, counts, expo, peaks, trios):
    groups = jnp.concatenate([near[...], far[...]], axis=0)
    wide = groups.astype(f32)
    norm = jnp.sum(wide * wide, axis=1, keepdims=True)
    zero = jnp.zeros((1, HALF), f32)
    blocks = []
    for c in range(2):
        product = lax.dot_general(groups, fresh[c], NT, preferred_element_type=f32)
        s = (2.0 * product - norm) / temper
        peak = jnp.max(s, axis=0, keepdims=True)
        part = jnp.exp(s - peak)
        expo[c], peaks[c] = part, peak
        total = jnp.sum(part, axis=0, keepdims=True)
        count = jnp.where(core[0] == c, counts[:, :HALF], zero)
        blocks += [peak, total, count, zero]
    block = jnp.concatenate(blocks, axis=0)
    for i in range(16):
        trios[i, :, :HALF] = block
        trios[i, :, HALF:] = jnp.zeros((8, 256 - HALF), f32)


def level_two_scores(core, fresh, near, far, counts):
    return pl.pallas_call(
        group_scores_kernel,
        in_specs=[SMEM] + [VMEM] * 4,
        out_specs=[VMEM] * 3,
        out_shape=[
            jax.ShapeDtypeStruct((2, 256, HALF), f32),
            jax.ShapeDtypeStruct((2, 1, HALF), f32),
            jax.ShapeDtypeStruct((16, 8, 256), f32),
        ],
        compiler_params=params(),
        cost_estimate=cost(2 * ROWS * 256 * D, 2 << 20, ROWS * 256),
    )(core, fresh, near, far, counts)


def group_sums_kernel(y_hi, expo, here, trios, fresh, out):
    sums, count = jnp.zeros((256, D), f32), jnp.zeros((256, 1), f32)
    for c in range(2):
        at = 4 * c
        peaks, totals = trios[:, at, :], trios[:, at + 1, :]
        peak = jnp.max(peaks, axis=0, keepdims=True)
        whole = jnp.sum(totals * jnp.exp(peaks - peak), axis=0, keepdims=True)
        counts = jnp.sum(trios[:, at + 2, :], axis=0, keepdims=True)
        peak, whole, counts = [v[:, :HALF] for v in (peak, whole, counts)]
        resp = (expo[c] * (jnp.exp(here[c] - peak) / whole)).astype(bf16)
        weighted = (counts * resp.astype(f32)).astype(bf16)
        sums = sums + lax.dot_general(weighted, fresh[c], NN, preferred_element_type=f32)
        count = count + jnp.sum(weighted.astype(f32), axis=1, keepdims=True)
    lanes = count_lanes(count)
    for place, at in ((y_hi[0], 0), (1 - y_hi[0], 128)):
        for i in range(16):
            block = slice(at + i * 8, at + i * 8 + 8)
            out[i, place, :, :D] = sums[block].astype(bf16)
            out[i, place, :, D:] = lanes[block]


def level_two_sums(y_hi, expo, here, trios, fresh):
    return pl.pallas_call(
        group_sums_kernel,
        in_specs=[SMEM] + [VMEM] * 4,
        out_specs=VMEM,
        out_shape=jax.ShapeDtypeStruct((16, 2, 8, WIDE), bf16),
        compiler_params=params(),
        cost_estimate=cost(2 * ROWS * 256 * D, 2 << 20, ROWS * 256),
    )(y_hi, expo, here, trios, fresh)


def groups_kernel(blocks, rows, out):
    sums, count = add_up(blocks, 32)
    new = ((sums + rows[...].astype(f32)) / (count + 1.0)).astype(bf16)
    for i in range(16):
        out[i] = new


def finish_groups(blocks, rows):
    return pl.pallas_call(
        groups_kernel,
        in_specs=[VMEM] * 2,
        out_specs=VMEM,
        out_shape=jax.ShapeDtypeStruct((16, 8, D), bf16),
        compiler_params=params(),
        cost_estimate=cost(1 << 19, 1 << 20),
    )(blocks, rows)


def exchange(blocks, axes):
    return lax.all_to_all(blocks, axes, 0, 0)


def ordered(first, mine, other):
    return jnp.where(first, mine, other), jnp.where(first, other, mine)


def cut(rows, at, n):
    return lax.dynamic_slice(rows, (at, 0), (n, rows.shape[1]), allow_negative_indices=False)


MIRROR = [(h * 4 + y, (1 - h) * 4 + 3 - y) for h in range(2) for y in range(4)]


def on_device(points, centroids, groups):
    core = lax.axis_index("core").astype(jnp.int32)
    y_hi = lax.axis_index("y_hi").astype(jnp.int32)
    z = lax.axis_index("z").astype(jnp.int32)
    cent = lax.axis_index(NEAR).astype(jnp.int32)
    odd = z % 2

    to_send = spread_halves(centroids.T)
    indices = (
        core[None],
        y_hi[None],
        z[None],
        (y_hi * 8 + z) * OWN,
        odd * (HALF - FAR),
        cent * 8,
        core == 0,
        y_hi == 0,
        odd == 0,
    )
    to_send, points, indices = lax.optimization_barrier((to_send, points, indices))
    core, y_hi, z, own_at, far_at, cent_at, first_core, first_y, even = indices
    piece_t = exchange(to_send, DP).reshape(D, ROWS)
    points_other = lax.ppermute(points, "core", SWAP)

    piece, scores_a, scores_b, pairs = level_one_scores(piece_t, points, points_other)
    mine = combine(exchange(pairs, NEAR))
    other = lax.ppermute(mine, "core", SWAP)
    blocks = level_one_sums(mine, other, scores_a, scores_b, points, points_other)
    rows = cut(piece, own_at, OWN)
    blocks, rows = lax.optimization_barrier((blocks, rows))
    blocks = exchange(blocks, CHIPS)
    fresh_rows, counts = finish_rows(z, blocks, rows)

    fresh_rows, groups_ready = lax.optimization_barrier((fresh_rows, groups))
    mine = exchange(fresh_rows, "z").reshape(HALF, D)
    groups_far = lax.ppermute(groups_ready, ("y_hi", "y_lo"), MIRROR)
    fresh = lax.all_gather(mine, "core")

    expo, here, trios = level_two_scores(core, fresh, groups, groups_far, counts)
    rest = HALF - FAR
    expo, mine = lax.optimization_barrier((expo, mine))
    part = cut(mine, far_at, FAR)
    part = lax.ppermute(part, "y_hi", SWAP)
    trios = exchange(trios, ("core", "z"))
    sums = level_two_sums(y_hi, expo, here, trios, fresh)
    sums, part = lax.optimization_barrier((sums, part))
    lacking = jnp.where(even, part[:rest], part[FAR - rest :])
    lacking = lax.ppermute(lacking, "z", [(i, i ^ 1) for i in range(8)])
    far_mine = jnp.where(
        even,
        jnp.concatenate([part, lacking], axis=0),
        jnp.concatenate([lacking, part], axis=0),
    )
    blocks = exchange(sums.reshape(32, 8, WIDE), (*NEAR, "y_hi"))
    rows = cut(groups, cent_at, 8)
    far_other = lax.ppermute(far_mine, "core", SWAP)
    far = ordered(first_core, far_mine, far_other)
    first, second = ordered(first_y, fresh[0], far[0]), ordered(first_y, fresh[1], far[1])
    fresh_all = jnp.concatenate([*first, *second], axis=0)
    blocks, fresh_all = lax.optimization_barrier((blocks, fresh_all))
    new_rows = finish_groups(blocks, rows)
    new_groups = exchange(new_rows, NEAR).reshape(128, D)
    return (fresh_all, new_groups)


def solution(mesh):
    split = Mesh(mesh.devices.reshape(2, 8, 2, 4, 4), ("y_hi", "z", "core", "y_lo", "x"))
    return jax.shard_map(
        on_device,
        mesh=split,
        in_specs=(P(DP, None), P(CENT, DP), P(DP, None)),
        out_specs=(P(CENT, None), P(DP, None)),
        check_vma=False,
    )
```

```python
import jax
import jax.numpy as jnp
from jax import lax
from jax.experimental import pallas as pl
from jax.experimental.pallas import tpu as pltpu
from jax.sharding import Mesh, PartitionSpec as P

temper = 20.0
f32, bf16 = jnp.float32, jnp.bfloat16
DP = ("y_hi", "z", "core")
CHIPS = ("y_hi", "z")
CENT = ("y_lo", "x")
NEAR = ("x", "y_lo")
SWAP = [(0, 1), (1, 0)]
D = 1024
WIDE = 1152
STEP = 512
ROWS = 384
OWN = 24
PACK = 200
FAR = 144
HALF = 192
VMEM = pl.BlockSpec(memory_space=pltpu.VMEM)
SMEM = pl.BlockSpec(memory_space=pltpu.SMEM)
NT = (((1,), (1,)), ((), ()))
NN = (((1,), (0,)), ((), ()))


def params(mib=8):
    return pltpu.CompilerParams(vmem_limit_bytes=mib * 1024 * 1024)


def cost(flops, nbytes, exps=0):
    return pl.CostEstimate(flops=flops, bytes_accessed=nbytes, transcendentals=exps)


def count_row(count):
    high = count.astype(bf16).astype(f32)
    mid = (count - high).astype(bf16).astype(f32)
    low = count - high - mid
    lane = lax.broadcasted_iota(jnp.int32, (OWN, 128), 1)
    row = lax.broadcasted_iota(jnp.int32, (OWN, 128), 0)
    placed = jnp.where(lane == row, high, 0.0)
    placed = jnp.where(lane == row + OWN, mid, placed)
    placed = jnp.where(lane == row + 2 * OWN, low, placed)
    return jnp.sum(placed, axis=0, keepdims=True)


def count_lanes(count):
    n = count.shape[0]
    high = count.astype(bf16).astype(f32)
    mid = (count - high).astype(bf16).astype(f32)
    low = count - high - mid
    lane = lax.broadcasted_iota(jnp.int32, (n, 128), 1)
    wide = jnp.where(lane == 0, high, jnp.where(lane == 1, mid, jnp.where(lane == 2, low, 0.0)))
    return wide.astype(bf16)


def add_up(blocks_ref, n):
    total = blocks_ref[0].astype(f32)
    for i in range(1, n):
        total = total + blocks_ref[i].astype(f32)
    count = jnp.sum(total[:, D:], axis=1, keepdims=True)
    return total[:, :D], count


def spread_kernel(columns, out):
    for i in range(32):
        out[i] = columns[:, (i % 2) * ROWS : (i % 2 + 1) * ROWS]


def spread_halves(columns):
    return pl.pallas_call(
        spread_kernel,
        in_specs=[VMEM],
        out_specs=VMEM,
        out_shape=jax.ShapeDtypeStruct((32, 32, ROWS), bf16),
        compiler_params=params(),
        cost_estimate=cost(0, 1 << 20),
    )(columns)


def scores_kernel(piece_t, points_a, points_b, piece, scores_a, scores_b, pairs):
    rows = piece_t[...].T
    piece[...] = rows
    wide = rows.astype(f32)
    norm = jnp.sum(wide * wide, axis=1, keepdims=True)
    for i in range(1024 // STEP):
        at = slice(i * STEP, (i + 1) * STEP)
        found = []
        for points, scores in ((points_a, scores_a), (points_b, scores_b)):
            product = lax.dot_general(piece[...], points[at, :], NT, preferred_element_type=f32)
            s = (2.0 * product - norm) * (1.0 / temper)
            scores[:, at] = s
            peak = jnp.max(s, axis=0, keepdims=True)
            found += [peak, jnp.sum(jnp.exp(s - peak), axis=0, keepdims=True)]
        block = jnp.concatenate(found, axis=0)
        for j in range(16):
            pairs[j, :, at] = block


def level_one_scores(piece_t, points_a, points_b):
    return pl.pallas_call(
        scores_kernel,
        in_specs=[VMEM] * 3,
        out_specs=[VMEM] * 4,
        out_shape=[
            jax.ShapeDtypeStruct((ROWS, D), bf16),
            jax.ShapeDtypeStruct((ROWS, 1024), f32),
            jax.ShapeDtypeStruct((ROWS, 1024), f32),
            jax.ShapeDtypeStruct((16, 4, 1024), f32),
        ],
        compiler_params=params(16),
        cost_estimate=cost(2 * ROWS * 2048 * D, 8 << 20, ROWS * 2048),
    )(piece_t, points_a, points_b)


def combine_kernel(pairs, out):
    for row in (0, 2):
        peaks, totals = pairs[:, row, :], pairs[:, row + 1, :]
        peak = jnp.max(peaks, axis=0, keepdims=True)
        out[row : row + 1, :] = peak
        out[row + 1 : row + 2, :] = jnp.sum(
            totals * jnp.exp(peaks - peak), axis=0, keepdims=True
        )


def combine(pairs):
    return pl.pallas_call(
        combine_kernel,
        in_specs=[VMEM],
        out_specs=VMEM,
        out_shape=jax.ShapeDtypeStruct((4, 1024), f32),
        compiler_params=params(),
        cost_estimate=cost(1 << 17, 1 << 18, 1 << 15),
    )(pairs)


def sums_kernel(mine, other, scores_a, scores_b, points_a, points_b, out, resp, total):
    count = jnp.zeros((ROWS, 1), f32)
    for place, scores, points in ((0, scores_a, points_a), (1, scores_b, points_b)):
        at = 2 * place
        peak_m, total_m = mine[at : at + 1, :], mine[at + 1 : at + 2, :]
        peak_o, total_o = other[2 - at : 3 - at, :], other[3 - at : 4 - at, :]
        peak = jnp.maximum(peak_m, peak_o)
        whole = total_m * jnp.exp(peak_m - peak) + total_o * jnp.exp(peak_o - peak)
        part = (jnp.exp(scores[...] - peak) * (1.0 / whole)).astype(bf16)
        resp[place] = part
        count = count + jnp.sum(part.astype(f32), axis=1, keepdims=True)
        for j in range(1024 // STEP):
            cols = slice(j * STEP, (j + 1) * STEP)
            sums = lax.dot_general(
                resp[place], points[:, cols], NN, preferred_element_type=f32
            )
            total[:, cols] = total[:, cols] + sums if place else sums
    for b in range(16):
        at = slice(b * OWN, (b + 1) * OWN)
        parts = [total[at, j * 128 : (j + 1) * 128] for j in range(8)]
        tail = jnp.zeros((7, 128), f32)
        out[b] = jnp.concatenate([*parts, count_row(count[at, :]), tail], axis=0).astype(bf16)


def level_one_sums(mine, other, scores_a, scores_b, points_a, points_b):
    return pl.pallas_call(
        sums_kernel,
        in_specs=[VMEM] * 6,
        out_specs=VMEM,
        out_shape=jax.ShapeDtypeStruct((16, PACK, 128), bf16),
        scratch_shapes=[pltpu.VMEM((2, ROWS, 1024), bf16), pltpu.VMEM((ROWS, D), f32)],
        compiler_params=params(24),
        cost_estimate=cost(2 * ROWS * 2048 * D, 8 << 20, ROWS * 2048),
    )(mine, other, scores_a, scores_b, points_a, points_b)


def fresh_kernel(z, blocks, rows, fresh, counts):
    total = blocks[0].astype(f32)
    for i in range(1, 16):
        total = total + blocks[i].astype(f32)
    sums = jnp.concatenate([total[j * OWN : (j + 1) * OWN] for j in range(8)], axis=1)
    lane = lax.broadcasted_iota(jnp.int32, (OWN, 128), 1)
    row = lax.broadcasted_iota(jnp.int32, (OWN, 128), 0)
    part = (lane == row) | (lane == row + OWN) | (lane == row + 2 * OWN)
    count = jnp.sum(jnp.where(part, total[192:193], 0.0), axis=1, keepdims=True)
    new = ((sums + rows[...].astype(f32)) / (count + 1.0)).astype(bf16)
    for i in range(8):
        fresh[i] = new
    lane = lax.broadcasted_iota(jnp.int32, (OWN, 256), 1)
    row = lax.broadcasted_iota(jnp.int32, (OWN, 256), 0)
    placed = jnp.where(lane == row + z[0] * OWN, count, 0.0)
    counts[...] = jnp.sum(placed, axis=0, keepdims=True)


def finish_rows(z, blocks, rows):
    return pl.pallas_call(
        fresh_kernel,
        in_specs=[SMEM, VMEM, VMEM],
        out_specs=[VMEM, VMEM],
        out_shape=[
            jax.ShapeDtypeStruct((8, OWN, D), bf16),
            jax.ShapeDtypeStruct((1, 256), f32),
        ],
        compiler_params=params(),
        cost_estimate=cost(1 << 19, 1 << 20),
    )(z, blocks, rows)


def group_scores_kernel(core, fresh, near, far, counts, expo, peaks, trios):
    groups = jnp.concatenate([near[...], far[...]], axis=0)
    wide = groups.astype(f32)
    norm = jnp.sum(wide * wide, axis=1, keepdims=True)
    zero = jnp.zeros((1, HALF), f32)
    blocks = []
    for c in range(2):
        product = lax.dot_general(groups, fresh[c], NT, preferred_element_type=f32)
        s = (2.0 * product - norm) / temper
        peak = jnp.max(s, axis=0, keepdims=True)
        part = jnp.exp(s - peak)
        expo[c], peaks[c] = part, peak
        total = jnp.sum(part, axis=0, keepdims=True)
        count = jnp.where(core[0] == c, counts[:, :HALF], zero)
        blocks += [peak, total, count, zero]
    block = jnp.concatenate(blocks, axis=0)
    for i in range(16):
        trios[i, :, :HALF] = block
        trios[i, :, HALF:] = jnp.zeros((8, 256 - HALF), f32)


def level_two_scores(core, fresh, near, far, counts):
    return pl.pallas_call(
        group_scores_kernel,
        in_specs=[SMEM] + [VMEM] * 4,
        out_specs=[VMEM] * 3,
        out_shape=[
            jax.ShapeDtypeStruct((2, 256, HALF), f32),
            jax.ShapeDtypeStruct((2, 1, HALF), f32),
            jax.ShapeDtypeStruct((16, 8, 256), f32),
        ],
        compiler_params=params(),
        cost_estimate=cost(2 * ROWS * 256 * D, 2 << 20, ROWS * 256),
    )(core, fresh, near, far, counts)


def group_sums_kernel(y_hi, expo, here, trios, fresh, out):
    sums, count = jnp.zeros((256, D), f32), jnp.zeros((256, 1), f32)
    for c in range(2):
        at = 4 * c
        peaks, totals = trios[:, at, :], trios[:, at + 1, :]
        peak = jnp.max(peaks, axis=0, keepdims=True)
        whole = jnp.sum(totals * jnp.exp(peaks - peak), axis=0, keepdims=True)
        counts = jnp.sum(trios[:, at + 2, :], axis=0, keepdims=True)
        peak, whole, counts = [v[:, :HALF] for v in (peak, whole, counts)]
        resp = (expo[c] * (jnp.exp(here[c] - peak) / whole)).astype(bf16)
        weighted = (counts * resp.astype(f32)).astype(bf16)
        sums = sums + lax.dot_general(weighted, fresh[c], NN, preferred_element_type=f32)
        count = count + jnp.sum(weighted.astype(f32), axis=1, keepdims=True)
    lanes = count_lanes(count)
    for place, at in ((y_hi[0], 0), (1 - y_hi[0], 128)):
        for i in range(16):
            block = slice(at + i * 8, at + i * 8 + 8)
            out[i, place, :, :D] = sums[block].astype(bf16)
            out[i, place, :, D:] = lanes[block]


def level_two_sums(y_hi, expo, here, trios, fresh):
    return pl.pallas_call(
        group_sums_kernel,
        in_specs=[SMEM] + [VMEM] * 4,
        out_specs=VMEM,
        out_shape=jax.ShapeDtypeStruct((16, 2, 8, WIDE), bf16),
        compiler_params=params(),
        cost_estimate=cost(2 * ROWS * 256 * D, 2 << 20, ROWS * 256),
    )(y_hi, expo, here, trios, fresh)


def groups_kernel(blocks, rows, out):
    sums, count = add_up(blocks, 32)
    new = ((sums + rows[...].astype(f32)) / (count + 1.0)).astype(bf16)
    for i in range(16):
        out[i] = new


def finish_groups(blocks, rows):
    return pl.pallas_call(
        groups_kernel,
        in_specs=[VMEM] * 2,
        out_specs=VMEM,
        out_shape=jax.ShapeDtypeStruct((16, 8, D), bf16),
        compiler_params=params(),
        cost_estimate=cost(1 << 19, 1 << 20),
    )(blocks, rows)


def exchange(blocks, axes):
    return lax.all_to_all(blocks, axes, 0, 0)


def ordered(first, mine, other):
    return jnp.where(first, mine, other), jnp.where(first, other, mine)


def cut(rows, at, n):
    return lax.dynamic_slice(rows, (at, 0), (n, rows.shape[1]), allow_negative_indices=False)


MIRROR = [(h * 4 + y, (1 - h) * 4 + 3 - y) for h in range(2) for y in range(4)]


def on_device(points, centroids, groups):
    core = lax.axis_index("core").astype(jnp.int32)
    y_hi = lax.axis_index("y_hi").astype(jnp.int32)
    z = lax.axis_index("z").astype(jnp.int32)
    cent = lax.axis_index(NEAR).astype(jnp.int32)
    odd = z % 2

    to_send = spread_halves(centroids.T)
    indices = (
        core[None],
        y_hi[None],
        z[None],
        (y_hi * 8 + z) * OWN,
        odd * (HALF - FAR),
        cent * 8,
        core == 0,
        y_hi == 0,
        odd == 0,
    )
    to_send, points, indices = lax.optimization_barrier((to_send, points, indices))
    core, y_hi, z, own_at, far_at, cent_at, first_core, first_y, even = indices
    piece_t = exchange(to_send, DP).reshape(D, ROWS)
    points_other = lax.ppermute(points, "core", SWAP)

    piece, scores_a, scores_b, pairs = level_one_scores(piece_t, points, points_other)
    mine = combine(exchange(pairs, NEAR))
    other = lax.ppermute(mine, "core", SWAP)
    blocks = level_one_sums(mine, other, scores_a, scores_b, points, points_other)
    rows = cut(piece, own_at, OWN)
    blocks, rows = lax.optimization_barrier((blocks, rows))
    blocks = exchange(blocks, CHIPS)
    fresh_rows, counts = finish_rows(z, blocks, rows)

    fresh_rows, groups_ready = lax.optimization_barrier((fresh_rows, groups))
    mine = exchange(fresh_rows, "z").reshape(HALF, D)
    groups_far = lax.ppermute(groups_ready, ("y_hi", "y_lo"), MIRROR)
    fresh = lax.all_gather(mine, "core")

    expo, here, trios = level_two_scores(core, fresh, groups, groups_far, counts)
    rest = HALF - FAR
    part = cut(mine, far_at, FAR)
    part = lax.ppermute(part, "y_hi", SWAP)
    trios = exchange(trios, ("core", "z"))
    sums = level_two_sums(y_hi, expo, here, trios, fresh)
    sums, part = lax.optimization_barrier((sums, part))
    lacking = jnp.where(even, part[:rest], part[FAR - rest :])
    lacking = lax.ppermute(lacking, "z", [(i, i ^ 1) for i in range(8)])
    far_mine = jnp.where(
        even,
        jnp.concatenate([part, lacking], axis=0),
        jnp.concatenate([lacking, part], axis=0),
    )
    blocks = exchange(sums.reshape(32, 8, WIDE), (*NEAR, "y_hi"))
    rows = cut(groups, cent_at, 8)
    far_other = lax.ppermute(far_mine, "core", SWAP)
    far = ordered(first_core, far_mine, far_other)
    first, second = ordered(first_y, fresh[0], far[0]), ordered(first_y, fresh[1], far[1])
    fresh_all = jnp.concatenate([*first, *second], axis=0)
    blocks, fresh_all = lax.optimization_barrier((blocks, fresh_all))
    new_rows = finish_groups(blocks, rows)
    new_groups = exchange(new_rows, NEAR).reshape(128, D)
    return (fresh_all, new_groups)


def solution(mesh):
    split = Mesh(mesh.devices.reshape(2, 8, 2, 4, 4), ("y_hi", "z", "core", "y_lo", "x"))
    return jax.shard_map(
        on_device,
        mesh=split,
        in_specs=(P(DP, None), P(CENT, DP), P(DP, None)),
        out_specs=(P(CENT, None), P(DP, None)),
        check_vma=False,
    )
```

```python
import jax
import jax.numpy as jnp
from jax import lax
from jax.experimental import pallas as pl
from jax.experimental.pallas import tpu as pltpu
from jax.sharding import Mesh, PartitionSpec as P

temper = 20.0
f32, bf16 = jnp.float32, jnp.bfloat16
DP = ("y_hi", "z", "core")
CHIPS = ("y_hi", "z")
CENT = ("y_lo", "x")
NEAR = ("x", "y_lo")
SWAP = [(0, 1), (1, 0)]
D = 1024
WIDE = 1152
STEP = 512
ROWS = 384
OWN = 24
PACK = 200
FAR = 144
HALF = 192
VMEM = pl.BlockSpec(memory_space=pltpu.VMEM)
SMEM = pl.BlockSpec(memory_space=pltpu.SMEM)
NT = (((1,), (1,)), ((), ()))
NN = (((1,), (0,)), ((), ()))


def params(mib=8):
    return pltpu.CompilerParams(vmem_limit_bytes=mib * 1024 * 1024)


def cost(flops, nbytes, exps=0):
    return pl.CostEstimate(flops=flops, bytes_accessed=nbytes, transcendentals=exps)


def count_row(count):
    high = count.astype(bf16).astype(f32)
    mid = (count - high).astype(bf16).astype(f32)
    low = count - high - mid
    lane = lax.broadcasted_iota(jnp.int32, (OWN, 128), 1)
    row = lax.broadcasted_iota(jnp.int32, (OWN, 128), 0)
    placed = jnp.where(lane == row, high, 0.0)
    placed = jnp.where(lane == row + OWN, mid, placed)
    placed = jnp.where(lane == row + 2 * OWN, low, placed)
    return jnp.sum(placed, axis=0, keepdims=True)


def count_lanes(count):
    n = count.shape[0]
    high = count.astype(bf16).astype(f32)
    mid = (count - high).astype(bf16).astype(f32)
    low = count - high - mid
    lane = lax.broadcasted_iota(jnp.int32, (n, 128), 1)
    wide = jnp.where(lane == 0, high, jnp.where(lane == 1, mid, jnp.where(lane == 2, low, 0.0)))
    return wide.astype(bf16)


def add_up(blocks_ref, n):
    total = blocks_ref[0].astype(f32)
    for i in range(1, n):
        total = total + blocks_ref[i].astype(f32)
    count = jnp.sum(total[:, D:], axis=1, keepdims=True)
    return total[:, :D], count


def spread_kernel(columns, out):
    for i in range(32):
        out[i] = columns[:, (i % 2) * ROWS : (i % 2 + 1) * ROWS]


def spread_halves(columns):
    return pl.pallas_call(
        spread_kernel,
        in_specs=[VMEM],
        out_specs=VMEM,
        out_shape=jax.ShapeDtypeStruct((32, 32, ROWS), bf16),
        compiler_params=params(),
        cost_estimate=cost(0, 1 << 20),
    )(columns)


def scores_kernel(piece_t, points_a, points_b, piece, scores_a, scores_b, pairs):
    rows = piece_t[...].T
    piece[...] = rows
    wide = rows.astype(f32)
    norm = jnp.sum(wide * wide, axis=1, keepdims=True)
    for i in range(1024 // STEP):
        at = slice(i * STEP, (i + 1) * STEP)
        found = []
        for points, scores in ((points_a, scores_a), (points_b, scores_b)):
            product = lax.dot_general(piece[...], points[at, :], NT, preferred_element_type=f32)
            s = (2.0 * product - norm) * (1.0 / temper)
            scores[:, at] = s
            peak = jnp.max(s, axis=0, keepdims=True)
            found += [peak, jnp.sum(jnp.exp(s - peak), axis=0, keepdims=True)]
        block = jnp.concatenate(found, axis=0)
        for j in range(16):
            pairs[j, :, at] = block


def level_one_scores(piece_t, points_a, points_b):
    return pl.pallas_call(
        scores_kernel,
        in_specs=[VMEM] * 3,
        out_specs=[VMEM] * 4,
        out_shape=[
            jax.ShapeDtypeStruct((ROWS, D), bf16),
            jax.ShapeDtypeStruct((ROWS, 1024), f32),
            jax.ShapeDtypeStruct((ROWS, 1024), f32),
            jax.ShapeDtypeStruct((16, 4, 1024), f32),
        ],
        compiler_params=params(16),
        cost_estimate=cost(2 * ROWS * 2048 * D, 8 << 20, ROWS * 2048),
    )(piece_t, points_a, points_b)


def combine_kernel(pairs, out):
    for row in (0, 2):
        peaks, totals = pairs[:, row, :], pairs[:, row + 1, :]
        peak = jnp.max(peaks, axis=0, keepdims=True)
        out[row : row + 1, :] = peak
        out[row + 1 : row + 2, :] = jnp.sum(
            totals * jnp.exp(peaks - peak), axis=0, keepdims=True
        )


def combine(pairs):
    return pl.pallas_call(
        combine_kernel,
        in_specs=[VMEM],
        out_specs=VMEM,
        out_shape=jax.ShapeDtypeStruct((4, 1024), f32),
        compiler_params=params(),
        cost_estimate=cost(1 << 17, 1 << 18, 1 << 15),
    )(pairs)


def sums_kernel(mine, other, scores_a, scores_b, points_a, points_b, out, resp, total):
    count = jnp.zeros((ROWS, 1), f32)
    for place, scores, points in ((0, scores_a, points_a), (1, scores_b, points_b)):
        at = 2 * place
        peak_m, total_m = mine[at : at + 1, :], mine[at + 1 : at + 2, :]
        peak_o, total_o = other[2 - at : 3 - at, :], other[3 - at : 4 - at, :]
        peak = jnp.maximum(peak_m, peak_o)
        whole = total_m * jnp.exp(peak_m - peak) + total_o * jnp.exp(peak_o - peak)
        part = (jnp.exp(scores[...] - peak) * (1.0 / whole)).astype(bf16)
        resp[place] = part
        count = count + jnp.sum(part.astype(f32), axis=1, keepdims=True)
        for j in range(1024 // STEP):
            cols = slice(j * STEP, (j + 1) * STEP)
            sums = lax.dot_general(
                resp[place], points[:, cols], NN, preferred_element_type=f32
            )
            total[:, cols] = total[:, cols] + sums if place else sums
    for b in range(16):
        at = slice(b * OWN, (b + 1) * OWN)
        parts = [total[at, j * 128 : (j + 1) * 128] for j in range(8)]
        tail = jnp.zeros((7, 128), f32)
        out[b] = jnp.concatenate([*parts, count_row(count[at, :]), tail], axis=0).astype(bf16)


def level_one_sums(mine, other, scores_a, scores_b, points_a, points_b):
    return pl.pallas_call(
        sums_kernel,
        in_specs=[VMEM] * 6,
        out_specs=VMEM,
        out_shape=jax.ShapeDtypeStruct((16, PACK, 128), bf16),
        scratch_shapes=[pltpu.VMEM((2, ROWS, 1024), bf16), pltpu.VMEM((ROWS, D), f32)],
        compiler_params=params(24),
        cost_estimate=cost(2 * ROWS * 2048 * D, 8 << 20, ROWS * 2048),
    )(mine, other, scores_a, scores_b, points_a, points_b)


def fresh_kernel(z, blocks, rows, fresh, counts):
    total = blocks[0].astype(f32)
    for i in range(1, 16):
        total = total + blocks[i].astype(f32)
    sums = jnp.concatenate([total[j * OWN : (j + 1) * OWN] for j in range(8)], axis=1)
    lane = lax.broadcasted_iota(jnp.int32, (OWN, 128), 1)
    row = lax.broadcasted_iota(jnp.int32, (OWN, 128), 0)
    part = (lane == row) | (lane == row + OWN) | (lane == row + 2 * OWN)
    count = jnp.sum(jnp.where(part, total[192:193], 0.0), axis=1, keepdims=True)
    new = ((sums + rows[...].astype(f32)) / (count + 1.0)).astype(bf16)
    for i in range(8):
        fresh[i] = new
    lane = lax.broadcasted_iota(jnp.int32, (OWN, 256), 1)
    row = lax.broadcasted_iota(jnp.int32, (OWN, 256), 0)
    placed = jnp.where(lane == row + z[0] * OWN, count, 0.0)
    counts[...] = jnp.sum(placed, axis=0, keepdims=True)


def finish_rows(z, blocks, rows):
    return pl.pallas_call(
        fresh_kernel,
        in_specs=[SMEM, VMEM, VMEM],
        out_specs=[VMEM, VMEM],
        out_shape=[
            jax.ShapeDtypeStruct((8, OWN, D), bf16),
            jax.ShapeDtypeStruct((1, 256), f32),
        ],
        compiler_params=params(),
        cost_estimate=cost(1 << 19, 1 << 20),
    )(z, blocks, rows)


def group_scores_kernel(core, fresh, near, far, counts, expo, peaks, trios):
    groups = jnp.concatenate([near[...], far[...]], axis=0)
    wide = groups.astype(f32)
    norm = jnp.sum(wide * wide, axis=1, keepdims=True)
    zero = jnp.zeros((1, HALF), f32)
    blocks = []
    for c in range(2):
        product = lax.dot_general(groups, fresh[c], NT, preferred_element_type=f32)
        s = (2.0 * product - norm) / temper
        peak = jnp.max(s, axis=0, keepdims=True)
        part = jnp.exp(s - peak)
        expo[c], peaks[c] = part, peak
        total = jnp.sum(part, axis=0, keepdims=True)
        count = jnp.where(core[0] == c, counts[:, :HALF], zero)
        blocks += [peak, total, count, zero]
    block = jnp.concatenate(blocks, axis=0)
    for i in range(16):
        trios[i, :, :HALF] = block
        trios[i, :, HALF:] = jnp.zeros((8, 256 - HALF), f32)


def level_two_scores(core, fresh, near, far, counts):
    return pl.pallas_call(
        group_scores_kernel,
        in_specs=[SMEM] + [VMEM] * 4,
        out_specs=[VMEM] * 3,
        out_shape=[
            jax.ShapeDtypeStruct((2, 256, HALF), f32),
            jax.ShapeDtypeStruct((2, 1, HALF), f32),
            jax.ShapeDtypeStruct((16, 8, 256), f32),
        ],
        compiler_params=params(),
        cost_estimate=cost(2 * ROWS * 256 * D, 2 << 20, ROWS * 256),
    )(core, fresh, near, far, counts)


def group_sums_kernel(y_hi, expo, here, trios, fresh, out):
    sums, count = jnp.zeros((256, D), f32), jnp.zeros((256, 1), f32)
    for c in range(2):
        at = 4 * c
        peaks, totals = trios[:, at, :], trios[:, at + 1, :]
        peak = jnp.max(peaks, axis=0, keepdims=True)
        whole = jnp.sum(totals * jnp.exp(peaks - peak), axis=0, keepdims=True)
        counts = jnp.sum(trios[:, at + 2, :], axis=0, keepdims=True)
        peak, whole, counts = [v[:, :HALF] for v in (peak, whole, counts)]
        resp = (expo[c] * (jnp.exp(here[c] - peak) / whole)).astype(bf16)
        weighted = (counts * resp.astype(f32)).astype(bf16)
        sums = sums + lax.dot_general(weighted, fresh[c], NN, preferred_element_type=f32)
        count = count + jnp.sum(weighted.astype(f32), axis=1, keepdims=True)
    lanes = count_lanes(count)
    for place, at in ((y_hi[0], 0), (1 - y_hi[0], 128)):
        for i in range(16):
            block = slice(at + i * 8, at + i * 8 + 8)
            out[i, place, :, :D] = sums[block].astype(bf16)
            out[i, place, :, D:] = lanes[block]


def level_two_sums(y_hi, expo, here, trios, fresh):
    return pl.pallas_call(
        group_sums_kernel,
        in_specs=[SMEM] + [VMEM] * 4,
        out_specs=VMEM,
        out_shape=jax.ShapeDtypeStruct((16, 2, 8, WIDE), bf16),
        compiler_params=params(),
        cost_estimate=cost(2 * ROWS * 256 * D, 2 << 20, ROWS * 256),
    )(y_hi, expo, here, trios, fresh)


def groups_kernel(blocks, rows, out):
    sums, count = add_up(blocks, 32)
    new = ((sums + rows[...].astype(f32)) / (count + 1.0)).astype(bf16)
    for i in range(16):
        out[i] = new


def finish_groups(blocks, rows):
    return pl.pallas_call(
        groups_kernel,
        in_specs=[VMEM] * 2,
        out_specs=VMEM,
        out_shape=jax.ShapeDtypeStruct((16, 8, D), bf16),
        compiler_params=params(),
        cost_estimate=cost(1 << 19, 1 << 20),
    )(blocks, rows)


def exchange(blocks, axes):
    return lax.all_to_all(blocks, axes, 0, 0)


def ordered(first, mine, other):
    return jnp.where(first, mine, other), jnp.where(first, other, mine)


def cut(rows, at, n):
    return lax.dynamic_slice(rows, (at, 0), (n, rows.shape[1]), allow_negative_indices=False)


MIRROR = [(h * 4 + y, (1 - h) * 4 + 3 - y) for h in range(2) for y in range(4)]


def on_device(points, centroids, groups):
    core = lax.axis_index("core").astype(jnp.int32)
    y_hi = lax.axis_index("y_hi").astype(jnp.int32)
    z = lax.axis_index("z").astype(jnp.int32)
    cent = lax.axis_index(NEAR).astype(jnp.int32)
    odd = z % 2

    to_send = spread_halves(centroids.T)
    indices = (
        core[None],
        y_hi[None],
        z[None],
        (y_hi * 8 + z) * OWN,
        odd * (HALF - FAR),
        cent * 8,
        core == 0,
        y_hi == 0,
        odd == 0,
    )
    to_send, points, indices = lax.optimization_barrier((to_send, points, indices))
    core, y_hi, z, own_at, far_at, cent_at, first_core, first_y, even = indices
    piece_t = exchange(to_send, DP).reshape(D, ROWS)
    points_other = lax.ppermute(points, "core", SWAP)

    piece, scores_a, scores_b, pairs = level_one_scores(piece_t, points, points_other)
    mine = combine(exchange(pairs, NEAR))
    other = lax.ppermute(mine, "core", SWAP)
    blocks = level_one_sums(mine, other, scores_a, scores_b, points, points_other)
    rows = cut(piece, own_at, OWN)
    blocks, rows = lax.optimization_barrier((blocks, rows))
    blocks = exchange(blocks, CHIPS)
    fresh_rows, counts = finish_rows(z, blocks, rows)

    fresh_rows, groups_ready = lax.optimization_barrier((fresh_rows, groups))
    mine = exchange(fresh_rows, "z").reshape(HALF, D)
    groups_far = lax.ppermute(groups_ready, ("y_hi", "y_lo"), MIRROR)
    fresh = lax.all_gather(mine, "core")

    expo, here, trios = level_two_scores(core, fresh, groups, groups_far, counts)
    rest = HALF - FAR
    expo, mine = lax.optimization_barrier((expo, mine))
    part = cut(mine, far_at, FAR)
    part = lax.ppermute(part, "y_hi", SWAP)
    trios = exchange(trios, ("core", "z"))
    sums = level_two_sums(y_hi, expo, here, trios, fresh)
    sums, part = lax.optimization_barrier((sums, part))
    lacking = jnp.where(even, part[:rest], part[FAR - rest :])
    lacking = lax.ppermute(lacking, "z", [(i, i ^ 1) for i in range(8)])
    far_mine = jnp.where(
        even,
        jnp.concatenate([part, lacking], axis=0),
        jnp.concatenate([lacking, part], axis=0),
    )
    blocks = exchange(sums.reshape(32, 8, WIDE), (*NEAR, "y_hi"))
    rows = cut(groups, cent_at, 8)
    far_other = lax.ppermute(far_mine, "core", SWAP)
    far = ordered(first_core, far_mine, far_other)
    first, second = ordered(first_y, fresh[0], far[0]), ordered(first_y, fresh[1], far[1])
    fresh_all = jnp.concatenate([*first, *second], axis=0)
    blocks, fresh_all = lax.optimization_barrier((blocks, fresh_all))
    new_rows = finish_groups(blocks, rows)
    new_groups = exchange(new_rows, NEAR).reshape(128, D)
    return (fresh_all, new_groups)


def solution(mesh):
    split = Mesh(mesh.devices.reshape(2, 8, 2, 4, 4), ("y_hi", "z", "core", "y_lo", "x"))
    return jax.shard_map(
        on_device,
        mesh=split,
        in_specs=(P(DP, None), P(CENT, DP), P(DP, None)),
        out_specs=(P(CENT, None), P(DP, None)),
        check_vma=False,
    )
```

```python
import jax
import jax.numpy as jnp
from jax import lax
from jax.experimental import pallas as pl
from jax.experimental.pallas import tpu as pltpu
from jax.sharding import Mesh, PartitionSpec as P

temper = 20.0
f32, bf16 = jnp.float32, jnp.bfloat16
DP = ("y_hi", "z", "core")
CHIPS = ("y_hi", "z")
CENT = ("y_lo", "x")
NEAR = ("x", "y_lo")
SWAP = [(0, 1), (1, 0)]
D = 1024
WIDE = 1152
STEP = 1024
ROWS = 384
OWN = 24
PACK = 200
FAR = 144
HALF = 192
VMEM = pl.BlockSpec(memory_space=pltpu.VMEM)
SMEM = pl.BlockSpec(memory_space=pltpu.SMEM)
NT = (((1,), (1,)), ((), ()))
NN = (((1,), (0,)), ((), ()))


def params(mib=8):
    return pltpu.CompilerParams(vmem_limit_bytes=mib * 1024 * 1024)


def cost(flops, nbytes, exps=0):
    return pl.CostEstimate(flops=flops, bytes_accessed=nbytes, transcendentals=exps)


def count_row(count):
    high = count.astype(bf16).astype(f32)
    mid = (count - high).astype(bf16).astype(f32)
    low = count - high - mid
    lane = lax.broadcasted_iota(jnp.int32, (OWN, 128), 1)
    row = lax.broadcasted_iota(jnp.int32, (OWN, 128), 0)
    placed = jnp.where(lane == row, high, 0.0)
    placed = jnp.where(lane == row + OWN, mid, placed)
    placed = jnp.where(lane == row + 2 * OWN, low, placed)
    return jnp.sum(placed, axis=0, keepdims=True)


def count_lanes(count):
    n = count.shape[0]
    high = count.astype(bf16).astype(f32)
    mid = (count - high).astype(bf16).astype(f32)
    low = count - high - mid
    lane = lax.broadcasted_iota(jnp.int32, (n, 128), 1)
    wide = jnp.where(lane == 0, high, jnp.where(lane == 1, mid, jnp.where(lane == 2, low, 0.0)))
    return wide.astype(bf16)


def add_up(blocks_ref, n):
    total = blocks_ref[0].astype(f32)
    for i in range(1, n):
        total = total + blocks_ref[i].astype(f32)
    count = jnp.sum(total[:, D:], axis=1, keepdims=True)
    return total[:, :D], count


def spread_kernel(columns, out):
    for i in range(32):
        out[i] = columns[:, (i % 2) * ROWS : (i % 2 + 1) * ROWS]


def spread_halves(columns):
    return pl.pallas_call(
        spread_kernel,
        in_specs=[VMEM],
        out_specs=VMEM,
        out_shape=jax.ShapeDtypeStruct((32, 32, ROWS), bf16),
        compiler_params=params(),
        cost_estimate=cost(0, 1 << 20),
    )(columns)


def scores_kernel(piece_t, points_a, points_b, piece, scores_a, scores_b, pairs):
    rows = piece_t[...].T
    piece[...] = rows
    wide = rows.astype(f32)
    norm = jnp.sum(wide * wide, axis=1, keepdims=True)
    for i in range(1024 // STEP):
        at = slice(i * STEP, (i + 1) * STEP)
        found = []
        for points, scores in ((points_a, scores_a), (points_b, scores_b)):
            product = lax.dot_general(piece[...], points[at, :], NT, preferred_element_type=f32)
            s = (2.0 * product - norm) * (1.0 / temper)
            scores[:, at] = s
            peak = jnp.max(s, axis=0, keepdims=True)
            found += [peak, jnp.sum(jnp.exp(s - peak), axis=0, keepdims=True)]
        block = jnp.concatenate(found, axis=0)
        for j in range(16):
            pairs[j, :, at] = block


def level_one_scores(piece_t, points_a, points_b):
    return pl.pallas_call(
        scores_kernel,
        in_specs=[VMEM] * 3,
        out_specs=[VMEM] * 4,
        out_shape=[
            jax.ShapeDtypeStruct((ROWS, D), bf16),
            jax.ShapeDtypeStruct((ROWS, 1024), f32),
            jax.ShapeDtypeStruct((ROWS, 1024), f32),
            jax.ShapeDtypeStruct((16, 4, 1024), f32),
        ],
        compiler_params=params(16),
        cost_estimate=cost(2 * ROWS * 2048 * D, 8 << 20, ROWS * 2048),
    )(piece_t, points_a, points_b)


def combine_kernel(pairs, out):
    for row in (0, 2):
        peaks, totals = pairs[:, row, :], pairs[:, row + 1, :]
        peak = jnp.max(peaks, axis=0, keepdims=True)
        out[row : row + 1, :] = peak
        out[row + 1 : row + 2, :] = jnp.sum(
            totals * jnp.exp(peaks - peak), axis=0, keepdims=True
        )


def combine(pairs):
    return pl.pallas_call(
        combine_kernel,
        in_specs=[VMEM],
        out_specs=VMEM,
        out_shape=jax.ShapeDtypeStruct((4, 1024), f32),
        compiler_params=params(),
        cost_estimate=cost(1 << 17, 1 << 18, 1 << 15),
    )(pairs)


def sums_kernel(mine, other, scores_a, scores_b, points_a, points_b, out, resp, total):
    count = jnp.zeros((ROWS, 1), f32)
    for place, scores, points in ((0, scores_a, points_a), (1, scores_b, points_b)):
        at = 2 * place
        peak_m, total_m = mine[at : at + 1, :], mine[at + 1 : at + 2, :]
        peak_o, total_o = other[2 - at : 3 - at, :], other[3 - at : 4 - at, :]
        peak = jnp.maximum(peak_m, peak_o)
        whole = total_m * jnp.exp(peak_m - peak) + total_o * jnp.exp(peak_o - peak)
        part = (jnp.exp(scores[...] - peak) * (1.0 / whole)).astype(bf16)
        resp[place] = part
        count = count + jnp.sum(part.astype(f32), axis=1, keepdims=True)
        for j in range(1024 // STEP):
            cols = slice(j * STEP, (j + 1) * STEP)
            sums = lax.dot_general(
                resp[place], points[:, cols], NN, preferred_element_type=f32
            )
            total[:, cols] = total[:, cols] + sums if place else sums
    for b in range(16):
        at = slice(b * OWN, (b + 1) * OWN)
        parts = [total[at, j * 128 : (j + 1) * 128] for j in range(8)]
        tail = jnp.zeros((7, 128), f32)
        out[b] = jnp.concatenate([*parts, count_row(count[at, :]), tail], axis=0).astype(bf16)


def level_one_sums(mine, other, scores_a, scores_b, points_a, points_b):
    return pl.pallas_call(
        sums_kernel,
        in_specs=[VMEM] * 6,
        out_specs=VMEM,
        out_shape=jax.ShapeDtypeStruct((16, PACK, 128), bf16),
        scratch_shapes=[pltpu.VMEM((2, ROWS, 1024), bf16), pltpu.VMEM((ROWS, D), f32)],
        compiler_params=params(24),
        cost_estimate=cost(2 * ROWS * 2048 * D, 8 << 20, ROWS * 2048),
    )(mine, other, scores_a, scores_b, points_a, points_b)


def fresh_kernel(z, blocks, rows, fresh, counts):
    total = blocks[0].astype(f32)
    for i in range(1, 16):
        total = total + blocks[i].astype(f32)
    sums = jnp.concatenate([total[j * OWN : (j + 1) * OWN] for j in range(8)], axis=1)
    lane = lax.broadcasted_iota(jnp.int32, (OWN, 128), 1)
    row = lax.broadcasted_iota(jnp.int32, (OWN, 128), 0)
    part = (lane == row) | (lane == row + OWN) | (lane == row + 2 * OWN)
    count = jnp.sum(jnp.where(part, total[192:193], 0.0), axis=1, keepdims=True)
    new = ((sums + rows[...].astype(f32)) / (count + 1.0)).astype(bf16)
    for i in range(8):
        fresh[i] = new
    lane = lax.broadcasted_iota(jnp.int32, (OWN, 256), 1)
    row = lax.broadcasted_iota(jnp.int32, (OWN, 256), 0)
    placed = jnp.where(lane == row + z[0] * OWN, count, 0.0)
    counts[...] = jnp.sum(placed, axis=0, keepdims=True)


def finish_rows(z, blocks, rows):
    return pl.pallas_call(
        fresh_kernel,
        in_specs=[SMEM, VMEM, VMEM],
        out_specs=[VMEM, VMEM],
        out_shape=[
            jax.ShapeDtypeStruct((8, OWN, D), bf16),
            jax.ShapeDtypeStruct((1, 256), f32),
        ],
        compiler_params=params(),
        cost_estimate=cost(1 << 19, 1 << 20),
    )(z, blocks, rows)


def group_scores_kernel(core, fresh, near, far, counts, expo, peaks, trios):
    groups = jnp.concatenate([near[...], far[...]], axis=0)
    wide = groups.astype(f32)
    norm = jnp.sum(wide * wide, axis=1, keepdims=True)
    zero = jnp.zeros((1, HALF), f32)
    blocks = []
    for c in range(2):
        product = lax.dot_general(groups, fresh[c], NT, preferred_element_type=f32)
        s = (2.0 * product - norm) / temper
        peak = jnp.max(s, axis=0, keepdims=True)
        part = jnp.exp(s - peak)
        expo[c], peaks[c] = part, peak
        total = jnp.sum(part, axis=0, keepdims=True)
        count = jnp.where(core[0] == c, counts[:, :HALF], zero)
        blocks += [peak, total, count, zero]
    block = jnp.concatenate(blocks, axis=0)
    for i in range(16):
        trios[i, :, :HALF] = block
        trios[i, :, HALF:] = jnp.zeros((8, 256 - HALF), f32)


def level_two_scores(core, fresh, near, far, counts):
    return pl.pallas_call(
        group_scores_kernel,
        in_specs=[SMEM] + [VMEM] * 4,
        out_specs=[VMEM] * 3,
        out_shape=[
            jax.ShapeDtypeStruct((2, 256, HALF), f32),
            jax.ShapeDtypeStruct((2, 1, HALF), f32),
            jax.ShapeDtypeStruct((16, 8, 256), f32),
        ],
        compiler_params=params(),
        cost_estimate=cost(2 * ROWS * 256 * D, 2 << 20, ROWS * 256),
    )(core, fresh, near, far, counts)


def group_sums_kernel(y_hi, expo, here, trios, fresh, out):
    sums, count = jnp.zeros((256, D), f32), jnp.zeros((256, 1), f32)
    for c in range(2):
        at = 4 * c
        peaks, totals = trios[:, at, :], trios[:, at + 1, :]
        peak = jnp.max(peaks, axis=0, keepdims=True)
        whole = jnp.sum(totals * jnp.exp(peaks - peak), axis=0, keepdims=True)
        counts = jnp.sum(trios[:, at + 2, :], axis=0, keepdims=True)
        peak, whole, counts = [v[:, :HALF] for v in (peak, whole, counts)]
        resp = (expo[c] * (jnp.exp(here[c] - peak) / whole)).astype(bf16)
        weighted = (counts * resp.astype(f32)).astype(bf16)
        sums = sums + lax.dot_general(weighted, fresh[c], NN, preferred_element_type=f32)
        count = count + jnp.sum(weighted.astype(f32), axis=1, keepdims=True)
    lanes = count_lanes(count)
    for place, at in ((y_hi[0], 0), (1 - y_hi[0], 128)):
        for i in range(16):
            block = slice(at + i * 8, at + i * 8 + 8)
            out[i, place, :, :D] = sums[block].astype(bf16)
            out[i, place, :, D:] = lanes[block]


def level_two_sums(y_hi, expo, here, trios, fresh):
    return pl.pallas_call(
        group_sums_kernel,
        in_specs=[SMEM] + [VMEM] * 4,
        out_specs=VMEM,
        out_shape=jax.ShapeDtypeStruct((16, 2, 8, WIDE), bf16),
        compiler_params=params(),
        cost_estimate=cost(2 * ROWS * 256 * D, 2 << 20, ROWS * 256),
    )(y_hi, expo, here, trios, fresh)


def groups_kernel(blocks, rows, out):
    sums, count = add_up(blocks, 32)
    new = ((sums + rows[...].astype(f32)) / (count + 1.0)).astype(bf16)
    for i in range(16):
        out[i] = new


def finish_groups(blocks, rows):
    return pl.pallas_call(
        groups_kernel,
        in_specs=[VMEM] * 2,
        out_specs=VMEM,
        out_shape=jax.ShapeDtypeStruct((16, 8, D), bf16),
        compiler_params=params(),
        cost_estimate=cost(1 << 19, 1 << 20),
    )(blocks, rows)


def exchange(blocks, axes):
    return lax.all_to_all(blocks, axes, 0, 0)


def ordered(first, mine, other):
    return jnp.where(first, mine, other), jnp.where(first, other, mine)


def cut(rows, at, n):
    return lax.dynamic_slice(rows, (at, 0), (n, rows.shape[1]), allow_negative_indices=False)


MIRROR = [(h * 4 + y, (1 - h) * 4 + 3 - y) for h in range(2) for y in range(4)]


def on_device(points, centroids, groups):
    core = lax.axis_index("core").astype(jnp.int32)
    y_hi = lax.axis_index("y_hi").astype(jnp.int32)
    z = lax.axis_index("z").astype(jnp.int32)
    cent = lax.axis_index(NEAR).astype(jnp.int32)
    odd = z % 2

    to_send = spread_halves(centroids.T)
    indices = (
        core[None],
        y_hi[None],
        z[None],
        (y_hi * 8 + z) * OWN,
        odd * (HALF - FAR),
        cent * 8,
        core == 0,
        y_hi == 0,
        odd == 0,
    )
    to_send, points, indices = lax.optimization_barrier((to_send, points, indices))
    core, y_hi, z, own_at, far_at, cent_at, first_core, first_y, even = indices
    piece_t = exchange(to_send, DP).reshape(D, ROWS)
    points_other = lax.ppermute(points, "core", SWAP)

    piece, scores_a, scores_b, pairs = level_one_scores(piece_t, points, points_other)
    mine = combine(exchange(pairs, NEAR))
    other = lax.ppermute(mine, "core", SWAP)
    blocks = level_one_sums(mine, other, scores_a, scores_b, points, points_other)
    rows = cut(piece, own_at, OWN)
    blocks, rows = lax.optimization_barrier((blocks, rows))
    blocks = exchange(blocks, CHIPS)
    fresh_rows, counts = finish_rows(z, blocks, rows)

    fresh_rows, groups_ready = lax.optimization_barrier((fresh_rows, groups))
    mine = exchange(fresh_rows, "z").reshape(HALF, D)
    groups_far = lax.ppermute(groups_ready, ("y_hi", "y_lo"), MIRROR)
    fresh = lax.all_gather(mine, "core")

    expo, here, trios = level_two_scores(core, fresh, groups, groups_far, counts)
    rest = HALF - FAR
    expo, mine = lax.optimization_barrier((expo, mine))
    part = cut(mine, far_at, FAR)
    part = lax.ppermute(part, "y_hi", SWAP)
    trios = exchange(trios, ("core", "z"))
    sums = level_two_sums(y_hi, expo, here, trios, fresh)
    sums, part = lax.optimization_barrier((sums, part))
    lacking = jnp.where(even, part[:rest], part[FAR - rest :])
    lacking = lax.ppermute(lacking, "z", [(i, i ^ 1) for i in range(8)])
    far_mine = jnp.where(
        even,
        jnp.concatenate([part, lacking], axis=0),
        jnp.concatenate([lacking, part], axis=0),
    )
    blocks = exchange(sums.reshape(32, 8, WIDE), (*NEAR, "y_hi"))
    rows = cut(groups, cent_at, 8)
    far_other = lax.ppermute(far_mine, "core", SWAP)
    far = ordered(first_core, far_mine, far_other)
    first, second = ordered(first_y, fresh[0], far[0]), ordered(first_y, fresh[1], far[1])
    fresh_all = jnp.concatenate([*first, *second], axis=0)
    blocks, fresh_all = lax.optimization_barrier((blocks, fresh_all))
    new_rows = finish_groups(blocks, rows)
    new_groups = exchange(new_rows, NEAR).reshape(128, D)
    return (fresh_all, new_groups)


def solution(mesh):
    split = Mesh(mesh.devices.reshape(2, 8, 2, 4, 4), ("y_hi", "z", "core", "y_lo", "x"))
    return jax.shard_map(
        on_device,
        mesh=split,
        in_specs=(P(DP, None), P(CENT, DP), P(DP, None)),
        out_specs=(P(CENT, None), P(DP, None)),
        check_vma=False,
    )
```
